256 devices in a mesh: cent: 16 (over y, x), pass: 16 (over z, core).
Axes of the slice: x: 4, y: 4, z: 8, core: 2. Of those that a mesh axis runs over, the one named last changes fastest.
Arguments:
- queries: bfloat16 [1024, 32, 128], P(('cent', 'pass')), may hold values from -6 to 6
- probes: int32 [1024, 4], replicated, may hold values from 0 to 262143
- centroids: bfloat16 [262144, 128], P('cent'), may hold values from -0.5 to 0.5
- codebook: float32 [4, 128], replicated, may hold values from -0.9 to 0.9
- token_cells: int32 [384, 30], P('pass'), may hold values from 0 to 262143
- codes: int32 [384, 2, 128], P('pass'), may hold values from 0 to 1073741823
- locations: int32 [384], replicated, may hold values from 0 to 383, as said below
- candidates: int32 [1024, 40], P(('cent', 'pass')), may hold values from 0 to 383, as said below
- lengths: int32 [1024], P(('cent', 'pass')), may hold values from 3 to 33
Outputs:
- top_scores: float32 [1024, 32], P(('cent', 'pass'))
- probe_scores: float32 [1024, 32, 4], P(('cent', 'pass'))
- maxsim: float32 [1024, 40], P(('cent', 'pass'))
The draws below stay inside these ranges and needn't reach their ends.
Inputs may be any that keep to these rules, and one draw needn't show every extreme that they name: A permutation: passage id i is stored by passage owner locations[i] // 24 at its slot locations[i] % 24. `candidates`: the first lengths[q] slots of query q hold distinct passage ids; at most 3 of them are stored by one passage owner, and for every query some owner stores exactly 3; later slots hold any passage ids.
All inputs are finite; a program needn't handle non-finite values.
Results may differ from the reference program's by a relative error of at most 0.00055.
Values may be sent and summed in bfloat16 or wider, within the bound.
A program may use at most 64 MiB of HBM per device.

```python
import math
import jax
import jax.numpy as jnp
from jax import lax

DIM = 128
QT = 32
NCENT = 262144
NQ = 1024
NPROBE = 4
PLEN = 30
P_OWN = 24
NPASS = 384
CAP = 3
CMAX = 40


def shared_plan(key):
    n_owner = NPASS // P_OWN
    keys = jax.random.split(jax.random.fold_in(key, 7), 7)
    locations = jax.random.permutation(keys[0], NPASS).astype(jnp.int32)
    inverse = jnp.argsort(locations, stable=True).astype(jnp.int32)
    hot_set = jax.random.permutation(keys[1], n_owner)[:2]
    hot_owner = hot_set[jax.random.randint(keys[2], (NQ,), 0, 2)]
    counts = jax.random.randint(keys[3], (NQ, n_owner), 0, CAP)
    query_index = jnp.arange(NQ)[:, None]
    counts = jnp.where(query_index == 0, CAP - 1, counts)
    counts = jnp.where(query_index == 1, 0, counts)
    counts = jnp.where(jnp.arange(n_owner)[None, :] == hot_owner[:, None], CAP, counts)
    slot_keys = jax.random.randint(keys[4], (NQ, n_owner, P_OWN), 0, 1 << 20) * P_OWN + jnp.arange(P_OWN)[None, None, :]
    chosen = jnp.argsort(slot_keys, axis=-1, stable=True)[:, :, :CAP].astype(jnp.int32)
    live_slots = jnp.arange(CAP)[None, None, :] < counts[:, :, None]
    positions = jnp.arange(n_owner)[None, :, None] * P_OWN + chosen
    passage_ids = inverse[positions].reshape(NQ, n_owner * CAP)
    filler = jax.random.randint(keys[5], (NQ, CMAX), 0, NPASS).astype(jnp.int32)
    every_id = jnp.concatenate([passage_ids, filler], axis=1)
    every_live = jnp.concatenate([live_slots.reshape(NQ, n_owner * CAP), jnp.zeros((NQ, CMAX), jnp.bool_)], axis=1)
    width_all = n_owner * CAP + CMAX
    ordering_keys = jax.random.randint(keys[6], (NQ, width_all), 0, 1 << 20) * width_all + jnp.arange(width_all)[None, :] + jnp.where(every_live, 0, 1 << 30)
    ordering = jnp.argsort(ordering_keys, axis=1, stable=True)[:, :CMAX]
    candidates = jnp.take_along_axis(every_id, ordering, axis=1).astype(jnp.int32)
    lengths = jnp.sum(live_slots.astype(jnp.int32), axis=(1, 2)).astype(jnp.int32)
    return (locations, candidates, lengths)


def draw_locations(key, part):
    return shared_plan(key)[0]


def draw_candidates(key, part):
    return shared_plan(key)[1]


def draw_lengths(key, part):
    return shared_plan(key)[2]


def place_ends(array, key, low, largest):
    dims = array.shape
    place = [jax.random.randint(jax.random.fold_in(key, axis), (), 0, dims[axis]) for axis in range(len(dims))]
    array = array.at[tuple(place)].set(low)
    longest = dims.index(max(dims))
    place[longest] = (place[longest] + 1) % dims[longest]
    return array.at[tuple(place)].set(largest)


def level_of(rng, shape, cuts, smallest, high):
    loudness = 1.0
    for position, shards_of in cuts:
        steps = jax.random.uniform(jax.random.fold_in(jax.random.fold_in(rng, 6), position), (shards_of,), jnp.float32, smallest / len(cuts), high / len(cuts))
        loudness = loudness * jnp.repeat(jnp.exp(steps), shape[position] // shards_of).reshape((-1,) + (1,) * (len(shape) - 1 - position))
    return loudness


def centred(rng, shape, deviation, bound, cuts=(), kind=jnp.bfloat16):
    loudness = level_of(rng, shape, cuts, -0.22, 0.18) if cuts else 1.0
    array = jax.random.normal(rng, shape, jnp.float32) * deviation * loudness
    return jnp.minimum(jnp.maximum(array, -bound), bound).astype(kind)


def setup_inputs(seed: int = 0) -> dict:
    splits = jax.random.split(jax.random.key(seed), 10)
    queries = centred(splits[0], (NQ, QT, DIM), 1.0, 6.0, ((0, 256),))
    probes = place_ends(jax.random.randint(splits[1], (NQ, NPROBE), 0, NCENT), jax.random.fold_in(splits[1], 1), 0, NCENT - 1).astype(jnp.int32)
    centroids = centred(splits[2], (NCENT, DIM), DIM ** -0.5, 0.5, ((0, 16),))
    codebook = centred(splits[3], (4, DIM), 0.15, 0.9, (), jnp.float32)
    token_cells = place_ends(jax.random.randint(splits[4], (NPASS, PLEN), 0, NCENT), jax.random.fold_in(splits[4], 1), 0, NCENT - 1).astype(jnp.int32)
    codes = place_ends(jax.random.randint(splits[5], (NPASS, PLEN // 15, DIM), 0, 1073741824), jax.random.fold_in(splits[5], 1), 0, 1073741823).astype(jnp.int32)
    locations = draw_locations(jax.random.fold_in(splits[9], 71), 0)
    candidates = draw_candidates(jax.random.fold_in(splits[9], 71), 0)
    lengths = draw_lengths(jax.random.fold_in(splits[9], 71), 0)
    return {"queries": queries, "probes": probes, "centroids": centroids, "codebook": codebook, "token_cells": token_cells, "codes": codes, "locations": locations, "candidates": candidates, "lengths": lengths}


def unpack_levels(codes):
    n_rows, n_groups, n_width = codes.shape
    shifts = 2 * jnp.arange(15, dtype=jnp.int32)
    levels = jnp.bitwise_and(jnp.right_shift(codes[:, :, None, :], shifts[None, None, :, None]), 3)
    return levels.reshape(n_rows, n_groups * 15, n_width)

def decode_store(cell_rows, levels, codebook):
    one_hot = (levels[..., None] == jnp.arange(4, dtype=jnp.int32)).astype(jnp.float32)
    residual = lax.optimization_barrier(jnp.sum(one_hot * jnp.transpose(codebook)[None, None, :, :], axis=-1))
    vector = cell_rows.astype(jnp.float32) + residual
    squares = lax.optimization_barrier(jnp.sum(vector * vector, axis=-1, keepdims=True))
    return (vector * lax.rsqrt(squares + 1e-06)).astype(jnp.bfloat16)

def reference(queries, probes, centroids, codebook, token_cells, codes, locations, candidates, lengths):
    flattened = queries.reshape(NQ * QT, DIM).astype(jnp.float32)
    block_size = math.gcd(NCENT, 8192)
    starts = jnp.arange(NCENT // block_size, dtype=jnp.int32) * block_size

    def block_max(offset):
        block_rows = lax.dynamic_slice_in_dim(centroids, offset, block_size, 0).astype(jnp.float32)
        return lax.optimization_barrier(jnp.max(jnp.dot(flattened, block_rows.T, precision=lax.Precision.HIGHEST), axis=1))
    top_scores = lax.optimization_barrier(jnp.max(lax.map(block_max, starts), axis=0)).reshape(NQ, QT)
    probe_rows = centroids[probes].astype(jnp.float32)
    probe_scores = jnp.einsum('qtd,qpd->qtp', queries.astype(jnp.float32), probe_rows, precision=lax.Precision.HIGHEST)
    stored = decode_store(centroids[token_cells], unpack_levels(codes), codebook)
    positions = locations[candidates]
    live_slots = jnp.arange(CMAX, dtype=jnp.int32)[None, :] < lengths[:, None]

    def one_query(pair):
        query_rows, where_rows = pair
        blocks = stored[where_rows].astype(jnp.float32)
        similarity = jnp.einsum('td,cjd->tcj', query_rows.astype(jnp.float32), blocks, precision=lax.Precision.HIGHEST)
        return lax.optimization_barrier(jnp.mean(lax.optimization_barrier(jnp.max(similarity, axis=2)), axis=0))
    mean_scores = lax.map(one_query, (queries, positions))
    maxsim = jnp.where(live_slots, mean_scores, 0.0)
    return (top_scores, probe_scores, maxsim)
```

```python
import jax
import jax.numpy as jnp
from jax import lax
from jax.experimental import pallas as pl
from jax.experimental.pallas import tpu as pltpu
from jax.sharding import PartitionSpec as P

MESH = pl.DeviceIdType.MESH
DIM = 128
QT = 32
NPROBE = 4
PLEN = 30
P_OWN = 24
CMAX = 40
NC = 16
NP = 16
QD = 4
TOK = QD * QT
SHARD = 16384
SHIFT = 14
CHUNK = 4096
TILE = 512
ROWS = 80
F32 = jnp.float32
BF16 = jnp.bfloat16


def ahead(c, d):
    y = lax.rem(lax.div(c, 4) + lax.div(d, 4), 4)
    x = lax.rem(lax.rem(c, 4) + lax.rem(d, 4), 4)
    return y * 4 + x


def behind(c, d):
    y = lax.rem(lax.div(c, 4) + 4 - lax.div(d, 4), 4)
    x = lax.rem(lax.rem(c, 4) + 4 - lax.rem(d, 4), 4)
    return y * 4 + x


def kernel(
    q_ref, probes, cells, codes, book, locations, candidates, lengths, cent_hbm,
    top_out, probe_out, score_out,
    cent, queries, row_send, row_recv, passages, sim_send, sim_recv, top_send, top_recv, where_at,
    load_sem, qs, qr, rs, rr, ps, pr, ss, sr, ts, tr,
):
    c = lax.axis_index("cent")
    p = lax.axis_index("pass")

    loads = [
        pltpu.make_async_copy(
            cent_hbm.at[pl.ds(i * CHUNK // 16, CHUNK // 16)], cent.at[pl.ds(i * CHUNK // 16, CHUNK // 16)], load_sem.at[i]
        )
        for i in range(SHARD // CHUNK)
    ]
    for load in loads:
        load.start()

    barrier = pltpu.get_barrier_semaphore()

    def greet(d, carry):
        pl.semaphore_signal(barrier, inc=1, device_id=(ahead(c, d), p), device_id_type=MESH)
        pl.semaphore_signal(barrier, inc=1, device_id=(c, lax.rem(p + d, NP)), device_id_type=MESH)
        return carry

    lax.fori_loop(1, 16, greet, 0)
    queries[pl.ds(0, TOK), :] = q_ref[...]

    lane8 = lax.broadcasted_iota(jnp.int32, (8, 128), 1)
    sub8 = lax.broadcasted_iota(jnp.int32, (8, 128), 0)
    for q in range(QD):
        found = jnp.full((8, 128), -1, jnp.int32)
        for slot in range(CMAX):
            found = jnp.where(lane8 == slot, locations[candidates[q, slot]], found)
        where_at[q] = jnp.where(lane8 < lengths[q], found, -1)

    pl.semaphore_wait(barrier, 30)

    def to_cent(src, dst, d, send, recv, target):
        return pltpu.make_async_remote_copy(
            src_ref=src, dst_ref=dst, send_sem=send.at[d], recv_sem=recv.at[d],
            device_id=(target, p), device_id_type=MESH,
        )

    def query_copy(d):
        return to_cent(
            queries.at[pl.ds(0, TOK)], queries.at[pl.ds(pl.multiple_of(d * TOK, TOK), TOK)], d, qs, qr, ahead(c, d)
        )

    def row_copy(d):
        return to_cent(row_send.at[d], row_recv.at[d], d, rs, rr, ahead(c, d))

    def passage_copy(d):
        return pltpu.make_async_remote_copy(
            src_ref=passages.at[0], dst_ref=passages.at[d], send_sem=ps.at[d], recv_sem=pr.at[d],
            device_id=(c, lax.rem(p + d, NP)), device_id_type=MESH,
        )

    def sim_copy(d):
        return to_cent(sim_send.at[d], sim_recv.at[d], d, ss, sr, behind(c, d))

    def top_copy(d):
        return to_cent(top_send.at[d], top_recv.at[d], d, ts, tr, behind(c, d))

    def send_queries(d, carry):
        query_copy(d).start()
        return carry

    lax.fori_loop(1, NC, send_queries, 0)
    for load in loads:
        load.wait()

    mine = [jnp.where(sub8 == r, c, -1) for r in range(8)]

    def pick(ids):
        parts = []
        for base in range(0, len(ids), 8):
            acc = jnp.zeros((8, DIM), F32)
            for r, i in enumerate(ids[base : base + 8]):
                pair = cent[(i & (SHARD - 1)) >> 4].astype(F32)
                ids_r = jnp.full((8, DIM), i, jnp.int32)
                half = jnp.where((ids_r & 8) != 0, pair[8:], pair[:8])
                row = jnp.take_along_axis(half, ids_r & 7, axis=0)
                acc = jnp.where(mine[r] == (ids_r >> SHIFT), row, acc)
            parts.append(acc)
        return jnp.concatenate(parts, axis=0).astype(BF16)

    def collect(d, carry):
        target = ahead(c, d)
        second = P_OWN - 8 + lax.div(target, 2)
        row_send[d, pl.ds(0, 32), :] = pick([cells[target, min(j, PLEN - 1)] for j in range(32)])
        row_send[d, pl.ds(32, 32), :] = pick([cells[second, min(j, PLEN - 1)] for j in range(32)])
        first = (target * NP + p) * QD
        row_send[d, pl.ds(64, 16), :] = pick([probes[k, first + q] for q in range(QD) for k in range(NPROBE)])

        @pl.when(d > 0)
        def _():
            row_copy(d).start()

        return carry

    lax.fori_loop(0, NC, collect, 0)

    def scan_tile(t, carry):
        tile = queries[pl.ds(pl.multiple_of(t * TILE, TILE), TILE), :]

        def step(i, best):
            rows = cent[pl.ds(i * (CHUNK // 16), CHUNK // 16)].reshape(CHUNK, DIM)
            dots = lax.dot_general(rows, tile, (((1,), (1,)), ((), ())), preferred_element_type=F32)
            return jnp.maximum(best, jnp.max(dots.reshape(CHUNK // 8, 8, TILE), axis=0))

        best = lax.fori_loop(0, SHARD // CHUNK, step, jnp.full((8, TILE), -jnp.inf, F32))
        for i in range(TILE // TOK):
            top_send[t * (TILE // TOK) + i] = best[:, i * TOK : (i + 1) * TOK]
        return carry

    def get_queries(d, carry):
        query_copy(d).wait_recv()
        return carry

    def send_tops(d, carry):
        top_copy(d).start()
        return carry

    lax.fori_loop(1, 4, get_queries, 0)
    scan_tile(0, 0)
    lax.fori_loop(1, 4, send_tops, 0)
    top_recv[0] = top_send[0]

    def get_rows(d, total):
        row_copy(d).wait_recv()
        return total + row_recv[d].astype(F32)

    rows = lax.fori_loop(1, NC, get_rows, row_send[0].astype(F32))
    own = queries[pl.ds(0, TOK), :]
    probe_dots = lax.dot_general(
        rows[64:].astype(BF16), own, (((1,), (1,)), ((), ())), preferred_element_type=F32
    )
    for q in range(QD):
        probe_out[q] = probe_dots[q * NPROBE : (q + 1) * NPROBE, q * QT : (q + 1) * QT]

    token = jnp.minimum(lax.broadcasted_iota(jnp.int32, (32, DIM), 0), PLEN - 1)
    shift = 2 * jnp.where(token >= 15, token - 15, token)
    for s, at in enumerate((c, P_OWN - 8 + lax.div(c, 2))):
        words = codes[at]
        word = jnp.where(token >= 15, words[1:2, :], words[0:1, :])
        level = jnp.right_shift(word, shift) & 3
        residual = jnp.where(
            level < 2,
            jnp.where(level == 0, book[0:1, :], book[1:2, :]),
            jnp.where(level == 2, book[2:3, :], book[3:4, :]),
        )
        vector = rows[s * 32 : (s + 1) * 32] + residual
        squares = jnp.sum(vector * vector, axis=-1, keepdims=True)
        passages[0, pl.ds(s * 32, 32), :] = (vector * lax.rsqrt(squares + 1e-06)).astype(BF16)

    def send_passages(d, carry):
        passage_copy(d).start()
        return carry

    lax.fori_loop(1, NP, send_passages, 0)

    lax.fori_loop(4, 8, get_queries, 0)
    scan_tile(1, 0)
    lax.fori_loop(4, 8, send_tops, 0)

    def get_passages(d, carry):
        passage_copy(d).wait_recv()
        return carry

    lax.fori_loop(1, NP, get_passages, 0)
    lax.fori_loop(8, NC, get_queries, 0)

    def sims(t, carry):
        tile = queries[pl.ds(pl.multiple_of(t * TILE, TILE), TILE), :]
        dots = lax.dot_general(
            passages[...].reshape(NP * 64, DIM), tile, (((1,), (1,)), ((), ())), preferred_element_type=F32
        )
        most = jnp.max(dots.reshape(32, 32, TILE), axis=1)
        for i in range(TILE // TOK):
            sim_send[t * (TILE // TOK) + i] = most[:, i * TOK : (i + 1) * TOK]
        return carry

    lax.fori_loop(0, NC * TOK // TILE, sims, 0)

    def send_sims(d, carry):
        sim_copy(d).start()
        return carry

    lax.fori_loop(1, NC, send_sims, 0)
    sim_recv[0] = sim_send[0]

    lax.fori_loop(2, 4, scan_tile, 0)
    lax.fori_loop(8, NC, send_tops, 0)

    def get_sims(d, carry):
        sim_copy(d).wait_recv()
        return carry

    lax.fori_loop(1, NC, get_sims, 0)
    groups = lax.broadcasted_iota(jnp.int32, (TOK, QD * 128), 0) // QT
    weights = jnp.where(
        groups == lax.broadcasted_iota(jnp.int32, (TOK, QD * 128), 1) // 128, 1.0 / QT, 0.0
    ).astype(BF16)
    odd = lax.rem(sub8, 2) == 1
    bases = []
    for g in range(4):
        owner = lax.rem(p + NP - (g * 4 + lax.div(sub8, 2)), NP)
        bases.append(owner * P_OWN)

    def score(d, totals):
        cc = ahead(c, d)
        m = sim_recv[d]
        high = m.astype(BF16)
        low = (m - high.astype(F32)).astype(BF16)
        means = jnp.dot(high, weights, preferred_element_type=F32) + jnp.dot(
            low, weights, preferred_element_type=F32
        )
        out = []
        for q in range(QD):
            total = totals[q]
            for g in range(4):
                position = bases[g] + jnp.where(odd, P_OWN - 8 + lax.div(cc, 2), cc)
                total = jnp.where(
                    position == where_at[q], means[g * 8 : (g + 1) * 8, q * 128 : (q + 1) * 128], total
                )
            out.append(total)
        return tuple(out)

    totals = lax.fori_loop(0, NC, score, tuple(jnp.zeros((8, 128), F32) for _ in range(QD)))
    for q in range(QD):
        score_out[pl.ds(q, 1), :] = jnp.sum(totals[q], axis=0, keepdims=True)[:, :CMAX]

    def get_tops(d, best):
        top_copy(d).wait_recv()
        return jnp.maximum(best, top_recv[d])

    best = lax.fori_loop(1, NC, get_tops, top_recv[0])
    best = jnp.max(best, axis=0, keepdims=True)
    for q in range(QD):
        top_out[pl.ds(q, 1), :] = best[:, q * QT : (q + 1) * QT]

    def finish(d, carry):
        query_copy(d).wait_send()
        row_copy(d).wait_send()
        passage_copy(d).wait_send()
        sim_copy(d).wait_send()
        top_copy(d).wait_send()
        return carry

    lax.fori_loop(1, NC, finish, 0)


def body(queries, probes, centroids, codebook, token_cells, codes, locations, candidates, lengths):
    vmem = pl.BlockSpec(memory_space=pltpu.VMEM)
    smem = pl.BlockSpec(memory_space=pltpu.SMEM)
    sems = pltpu.SemaphoreType.DMA((NC,))
    top, probe, score = pl.pallas_call(
        kernel,
        out_shape=(
            jax.ShapeDtypeStruct((QD, QT), F32),
            jax.ShapeDtypeStruct((QD, NPROBE, QT), F32),
            jax.ShapeDtypeStruct((QD, CMAX), F32),
        ),
        in_specs=[vmem, smem, smem, vmem, vmem, smem, smem, smem, pl.BlockSpec(memory_space=pl.ANY)],
        out_specs=(vmem, vmem, vmem),
        scratch_shapes=[
            pltpu.VMEM((SHARD // 16, 16, DIM), BF16),
            pltpu.VMEM((NC * TOK, DIM), BF16),
            pltpu.VMEM((NC, ROWS, DIM), BF16),
            pltpu.VMEM((NC, ROWS, DIM), BF16),
            pltpu.VMEM((NP, 64, DIM), BF16),
            pltpu.VMEM((NC, 32, TOK), F32),
            pltpu.VMEM((NC, 32, TOK), F32),
            pltpu.VMEM((NC, 8, TOK), F32),
            pltpu.VMEM((NC, 8, TOK), F32),
            pltpu.VMEM((QD, 8, 128), jnp.int32),
            pltpu.SemaphoreType.DMA((SHARD // CHUNK,)),
        ]
        + [sems] * 10,
        compiler_params=pltpu.CompilerParams(
            collective_id=0, has_side_effects=True, vmem_limit_bytes=48 << 20
        ),
        name="late_interaction",
    )(
        queries.reshape(TOK, DIM), probes.T, token_cells, codes, codebook, locations, candidates, lengths,
        centroids.reshape(SHARD // 16, 16, DIM),
    )
    return top, jnp.transpose(probe, (0, 2, 1)), score


def solution(mesh):
    placed = (
        P(("cent", "pass"), None, None),
        P(),
        P("cent", None),
        P(),
        P("pass", None),
        P("pass", None, None),
        P(),
        P(("cent", "pass"), None),
        P(("cent", "pass")),
    )
    return jax.shard_map(
        body,
        mesh=mesh,
        in_specs=placed,
        out_specs=(
            P(("cent", "pass"), None),
            P(("cent", "pass"), None, None),
            P(("cent", "pass"), None),
        ),
        check_vma=False,
    )
```

```python
import jax
import jax.numpy as jnp
from jax import lax
from jax.experimental import pallas as pl
from jax.experimental.pallas import tpu as pltpu
from jax.sharding import PartitionSpec as P

MESH = pl.DeviceIdType.MESH
DIM = 128
QT = 32
NPROBE = 4
PLEN = 30
P_OWN = 24
CMAX = 40
NC = 16
NP = 16
QD = 4
TOK = QD * QT
SHARD = 16384
SHIFT = 14
CHUNK = 4096
TILE = 512
ROWS = 80
F32 = jnp.float32
BF16 = jnp.bfloat16


def ahead(c, d):
    y = lax.rem(lax.div(c, 4) + lax.div(d, 4), 4)
    x = lax.rem(lax.rem(c, 4) + lax.rem(d, 4), 4)
    return y * 4 + x


def behind(c, d):
    y = lax.rem(lax.div(c, 4) + 4 - lax.div(d, 4), 4)
    x = lax.rem(lax.rem(c, 4) + 4 - lax.rem(d, 4), 4)
    return y * 4 + x


def kernel(
    q_hbm, probes_hbm, cells_hbm, codes_hbm, book_hbm, locations_hbm, candidates_hbm, lengths_hbm, cent_hbm,
    top_out, probe_out, score_out,
    probes, cells, codes, book, locations, candidates, lengths,
    cent, queries, row_send, row_recv, passages, sim_send, sim_recv, top_send, top_recv, where_at,
    load_sem, small_sem, qs, qr, rs, rr, ps, pr, ss, sr, ts, tr,
):
    c = lax.axis_index("cent")
    p = lax.axis_index("pass")

    loads = [
        pltpu.make_async_copy(
            cent_hbm.at[pl.ds(i * CHUNK // 16, CHUNK // 16)], cent.at[pl.ds(i * CHUNK // 16, CHUNK // 16)], load_sem.at[i]
        )
        for i in range(SHARD // CHUNK)
    ]
    small = [
        pltpu.make_async_copy(src, dst, small_sem.at[i])
        for i, (src, dst) in enumerate(
            (
                (q_hbm, queries.at[pl.ds(0, TOK)]),
                (cells_hbm, cells),
                (probes_hbm, probes),
                (codes_hbm, codes),
                (book_hbm, book),
                (locations_hbm, locations),
                (candidates_hbm, candidates),
                (lengths_hbm, lengths),
            )
        )
    ]
    for load in small + loads:
        load.start()

    barrier = pltpu.get_barrier_semaphore()

    def greet(d, carry):
        pl.semaphore_signal(barrier, inc=1, device_id=(ahead(c, d), p), device_id_type=MESH)
        pl.semaphore_signal(barrier, inc=1, device_id=(c, lax.rem(p + d, NP)), device_id_type=MESH)
        return carry

    lax.fori_loop(1, 16, greet, 0)

    pl.semaphore_wait(barrier, 30)

    for load in small:
        load.wait()
    sub8 = lax.broadcasted_iota(jnp.int32, (8, 128), 0)

    def to_cent(src, dst, d, send, recv, target):
        return pltpu.make_async_remote_copy(
            src_ref=src, dst_ref=dst, send_sem=send.at[d], recv_sem=recv.at[d],
            device_id=(target, p), device_id_type=MESH,
        )

    def query_copy(d):
        return to_cent(
            queries.at[pl.ds(0, TOK)], queries.at[pl.ds(pl.multiple_of(d * TOK, TOK), TOK)], d, qs, qr, ahead(c, d)
        )

    def row_copy(d):
        return to_cent(row_send.at[d], row_recv.at[d], d, rs, rr, ahead(c, d))

    def passage_copy(d):
        return pltpu.make_async_remote_copy(
            src_ref=passages.at[0], dst_ref=passages.at[d], send_sem=ps.at[d], recv_sem=pr.at[d],
            device_id=(c, lax.rem(p + d, NP)), device_id_type=MESH,
        )

    def sim_copy(d):
        return to_cent(sim_send.at[d], sim_recv.at[d], d, ss, sr, behind(c, d))

    def top_copy(d):
        return to_cent(top_send.at[d], top_recv.at[d], d, ts, tr, behind(c, d))

    def send_queries(d, carry):
        query_copy(d).start()
        return carry

    lax.fori_loop(1, 4, send_queries, 0)
    for load in loads:
        load.wait()

    mine = [jnp.where(sub8 == r, c, -1) for r in range(8)]

    def pick(ids):
        parts = []
        for base in range(0, len(ids), 8):
            acc = jnp.zeros((8, DIM), F32)
            for r, i in enumerate(ids[base : base + 8]):
                pair = cent[(i & (SHARD - 1)) >> 4].astype(F32)
                ids_r = jnp.full((8, DIM), i, jnp.int32)
                half = jnp.where((ids_r & 8) != 0, pair[8:], pair[:8])
                row = jnp.take_along_axis(half, ids_r & 7, axis=0)
                acc = jnp.where(mine[r] == (ids_r >> SHIFT), row, acc)
            parts.append(acc)
        return jnp.concatenate(parts, axis=0).astype(BF16)

    def collect(d, carry):
        target = ahead(c, d)
        second = P_OWN - 8 + lax.div(target, 2)
        row_send[d, pl.ds(0, 32), :] = pick([cells[target, min(j, PLEN - 1)] for j in range(32)])
        row_send[d, pl.ds(32, 32), :] = pick([cells[second, min(j, PLEN - 1)] for j in range(32)])
        first = (target * NP + p) * QD
        row_send[d, pl.ds(64, 16), :] = pick([probes[k, first + q] for q in range(QD) for k in range(NPROBE)])

        @pl.when(d > 0)
        def _():
            row_copy(d).start()

        return carry

    lax.fori_loop(0, NC, collect, 0)
    lax.fori_loop(4, NC, send_queries, 0)

    lane8 = lax.broadcasted_iota(jnp.int32, (8, 128), 1)
    for q in range(QD):
        found = jnp.full((8, 128), -1, jnp.int32)
        for slot in range(CMAX):
            found = jnp.where(lane8 == slot, locations[candidates[q, slot]], found)
        where_at[q] = jnp.where(lane8 < lengths[q], found, -1)

    def scan_tile(t, carry):
        tile = queries[pl.ds(pl.multiple_of(t * TILE, TILE), TILE), :]

        def step(i, best):
            rows = cent[pl.ds(i * (CHUNK // 16), CHUNK // 16)].reshape(CHUNK, DIM)
            dots = lax.dot_general(rows, tile, (((1,), (1,)), ((), ())), preferred_element_type=F32)
            return jnp.maximum(best, jnp.max(dots.reshape(CHUNK // 8, 8, TILE), axis=0))

        best = lax.fori_loop(0, SHARD // CHUNK, step, jnp.full((8, TILE), -jnp.inf, F32))
        for i in range(TILE // TOK):
            top_send[t * (TILE // TOK) + i] = best[:, i * TOK : (i + 1) * TOK]
        return carry

    def get_queries(d, carry):
        query_copy(d).wait_recv()
        return carry

    def send_tops(d, carry):
        top_copy(d).start()
        return carry

    lax.fori_loop(1, 4, get_queries, 0)
    scan_tile(0, 0)
    lax.fori_loop(1, 4, send_tops, 0)
    top_recv[0] = top_send[0]

    def get_rows(d, total):
        row_copy(d).wait_recv()
        return total + row_recv[d].astype(F32)

    rows = lax.fori_loop(1, NC, get_rows, row_send[0].astype(F32))
    own = queries[pl.ds(0, TOK), :]
    probe_dots = lax.dot_general(
        rows[64:].astype(BF16), own, (((1,), (1,)), ((), ())), preferred_element_type=F32
    )
    for q in range(QD):
        probe_out[q] = probe_dots[q * NPROBE : (q + 1) * NPROBE, q * QT : (q + 1) * QT]

    token = jnp.minimum(lax.broadcasted_iota(jnp.int32, (32, DIM), 0), PLEN - 1)
    shift = 2 * jnp.where(token >= 15, token - 15, token)
    for s, at in enumerate((c, P_OWN - 8 + lax.div(c, 2))):
        words = codes[at]
        word = jnp.where(token >= 15, words[1:2, :], words[0:1, :])
        level = jnp.right_shift(word, shift) & 3
        residual = jnp.where(
            level < 2,
            jnp.where(level == 0, book[0:1, :], book[1:2, :]),
            jnp.where(level == 2, book[2:3, :], book[3:4, :]),
        )
        vector = rows[s * 32 : (s + 1) * 32] + residual
        squares = jnp.sum(vector * vector, axis=-1, keepdims=True)
        passages[0, pl.ds(s * 32, 32), :] = (vector * lax.rsqrt(squares + 1e-06)).astype(BF16)

    def send_passages(d, carry):
        passage_copy(d).start()
        return carry

    lax.fori_loop(1, NP, send_passages, 0)

    lax.fori_loop(4, 8, get_queries, 0)
    scan_tile(1, 0)
    lax.fori_loop(4, 8, send_tops, 0)

    lax.fori_loop(8, 12, get_queries, 0)
    scan_tile(2, 0)
    lax.fori_loop(8, 12, send_tops, 0)

    def get_passages(d, carry):
        passage_copy(d).wait_recv()
        return carry

    lax.fori_loop(1, NP, get_passages, 0)
    lax.fori_loop(12, NC, get_queries, 0)

    def sims(t, carry):
        tile = queries[pl.ds(pl.multiple_of(t * TILE, TILE), TILE), :]
        dots = lax.dot_general(
            passages[...].reshape(NP * 64, DIM), tile, (((1,), (1,)), ((), ())), preferred_element_type=F32
        )
        most = jnp.max(dots.reshape(32, 32, TILE), axis=1)
        for i in range(TILE // TOK):
            sim_send[t * (TILE // TOK) + i] = most[:, i * TOK : (i + 1) * TOK]
        return carry

    lax.fori_loop(0, NC * TOK // TILE, sims, 0)

    def send_sims(d, carry):
        sim_copy(d).start()
        return carry

    lax.fori_loop(1, NC, send_sims, 0)
    sim_recv[0] = sim_send[0]

    scan_tile(3, 0)
    lax.fori_loop(12, NC, send_tops, 0)

    def get_sims(d, carry):
        sim_copy(d).wait_recv()
        return carry

    lax.fori_loop(1, NC, get_sims, 0)
    groups = lax.broadcasted_iota(jnp.int32, (TOK, QD * 128), 0) // QT
    weights = jnp.where(
        groups == lax.broadcasted_iota(jnp.int32, (TOK, QD * 128), 1) // 128, 1.0 / QT, 0.0
    ).astype(BF16)
    odd = lax.rem(sub8, 2) == 1
    bases = []
    for g in range(4):
        owner = lax.rem(p + NP - (g * 4 + lax.div(sub8, 2)), NP)
        bases.append(owner * P_OWN)

    def score(d, totals):
        cc = ahead(c, d)
        m = sim_recv[d]
        high = m.astype(BF16)
        low = (m - high.astype(F32)).astype(BF16)
        means = jnp.dot(high, weights, preferred_element_type=F32) + jnp.dot(
            low, weights, preferred_element_type=F32
        )
        out = []
        for q in range(QD):
            total = totals[q]
            for g in range(4):
                position = bases[g] + jnp.where(odd, P_OWN - 8 + lax.div(cc, 2), cc)
                total = jnp.where(
                    position == where_at[q], means[g * 8 : (g + 1) * 8, q * 128 : (q + 1) * 128], total
                )
            out.append(total)
        return tuple(out)

    totals = lax.fori_loop(0, NC, score, tuple(jnp.zeros((8, 128), F32) for _ in range(QD)))
    for q in range(QD):
        score_out[pl.ds(q, 1), :] = jnp.sum(totals[q], axis=0, keepdims=True)[:, :CMAX]

    def get_tops(d, best):
        top_copy(d).wait_recv()
        return jnp.maximum(best, top_recv[d])

    best = lax.fori_loop(1, NC, get_tops, top_recv[0])
    best = jnp.max(best, axis=0, keepdims=True)
    for q in range(QD):
        top_out[pl.ds(q, 1), :] = best[:, q * QT : (q + 1) * QT]

    def finish(d, carry):
        query_copy(d).wait_send()
        row_copy(d).wait_send()
        passage_copy(d).wait_send()
        sim_copy(d).wait_send()
        top_copy(d).wait_send()
        return carry

    lax.fori_loop(1, NC, finish, 0)


def deliver(top, probe, score, top_out, probe_out, score_out):
    top_out[...] = top[...]
    probe_out[...] = probe[...]
    score_out[...] = score[...]


def body(queries, probes, centroids, codebook, token_cells, codes, locations, candidates, lengths):
    vmem = pl.BlockSpec(memory_space=pltpu.VMEM)
    sems = pltpu.SemaphoreType.DMA((NC,))
    results = pl.pallas_call(
        kernel,
        out_shape=(
            jax.ShapeDtypeStruct((QD, QT), F32),
            jax.ShapeDtypeStruct((QD, NPROBE, QT), F32),
            jax.ShapeDtypeStruct((QD, CMAX), F32),
        ),
        in_specs=[pl.BlockSpec(memory_space=pltpu.HBM)] * 9,
        out_specs=(vmem, vmem, vmem),
        scratch_shapes=[
            pltpu.SMEM((NPROBE, NC * NP * QD), jnp.int32),
            pltpu.SMEM((P_OWN, PLEN), jnp.int32),
            pltpu.VMEM((P_OWN, 2, DIM), jnp.int32),
            pltpu.VMEM((4, DIM), F32),
            pltpu.SMEM((NP * P_OWN,), jnp.int32),
            pltpu.SMEM((QD, CMAX), jnp.int32),
            pltpu.SMEM((QD,), jnp.int32),
            pltpu.VMEM((SHARD // 16, 16, DIM), BF16),
            pltpu.VMEM((NC * TOK, DIM), BF16),
            pltpu.VMEM((NC, ROWS, DIM), BF16),
            pltpu.VMEM((NC, ROWS, DIM), BF16),
            pltpu.VMEM((NP, 64, DIM), BF16),
            pltpu.VMEM((NC, 32, TOK), F32),
            pltpu.VMEM((NC, 32, TOK), F32),
            pltpu.VMEM((NC, 8, TOK), F32),
            pltpu.VMEM((NC, 8, TOK), F32),
            pltpu.VMEM((QD, 8, 128), jnp.int32),
            pltpu.SemaphoreType.DMA((SHARD // CHUNK,)),
            pltpu.SemaphoreType.DMA((8,)),
        ]
        + [sems] * 10,
        compiler_params=pltpu.CompilerParams(
            collective_id=0, has_side_effects=True, vmem_limit_bytes=60 << 20
        ),
        name="late_interaction",
    )(
        queries.reshape(TOK, DIM), probes.T, token_cells, codes, codebook, locations, candidates, lengths,
        centroids.reshape(SHARD // 16, 16, DIM),
    )
    top, probe, score = pl.pallas_call(
        deliver,
        out_shape=tuple(jax.ShapeDtypeStruct(r.shape, r.dtype) for r in results),
        in_specs=[vmem] * 3,
        out_specs=[vmem] * 3,
        name="deliver",
    )(*results)
    return top, jnp.transpose(probe, (0, 2, 1)), score


def solution(mesh):
    placed = (
        P(("cent", "pass"), None, None),
        P(),
        P("cent", None),
        P(),
        P("pass", None),
        P("pass", None, None),
        P(),
        P(("cent", "pass"), None),
        P(("cent", "pass")),
    )
    return jax.shard_map(
        body,
        mesh=mesh,
        in_specs=placed,
        out_specs=(
            P(("cent", "pass"), None),
            P(("cent", "pass"), None, None),
            P(("cent", "pass"), None),
        ),
        check_vma=False,
    )
```

```python
import jax
import jax.numpy as jnp
from jax import lax
from jax.experimental import pallas as pl
from jax.experimental.pallas import tpu as pltpu
from jax.sharding import PartitionSpec as P

MESH = pl.DeviceIdType.MESH
DIM = 128
QT = 32
NPROBE = 4
PLEN = 30
P_OWN = 24
CMAX = 40
NC = 16
NP = 16
QD = 4
TOK = QD * QT
SHARD = 16384
SHIFT = 14
CHUNK = 4096
TILE = 512
STEPS = SHARD // CHUNK
EVEN = 8 * 64
F32 = jnp.float32
BF16 = jnp.bfloat16


def kernel(
    q_hbm, probes_hbm, cells_hbm, codes_hbm, book_hbm, locations_hbm, candidates_hbm, lengths_hbm, cent_hbm,
    top_out, probe_out, score_out,
    probes, cells, codes, book, locations, candidates, lengths,
    cent, queries, first_send, first_recv, second_send, second_recv, column_send, column_recv, late_send, late_recv,
    probed, passages, result_send, result_recv, wanted, running,
    load_sem, small_sem, qs, qr, ws, wr, vs, vr, us, ur,
):
    c = lax.axis_index("cent")
    p = lax.axis_index("pass")
    y, x = lax.div(c, 4), lax.rem(c, 4)
    z, core = lax.div(p, 2), lax.rem(p, 2)
    odd = lax.rem(c + p, 2)
    second_of = P_OWN - 8 + lax.div(c, 2)

    def cent_at(dy, dx):
        return lax.rem(y + dy, 4) * 4 + lax.rem(x + dx, 4)

    def pass_at(dz):
        return lax.rem(z + dz, 8) * 2 + core

    other = z * 2 + 1 - core

    loads = [
        pltpu.make_async_copy(
            cent_hbm.at[pl.ds(i * CHUNK // 16, CHUNK // 16)], cent.at[pl.ds(i * CHUNK // 16, CHUNK // 16)], load_sem.at[i]
        )
        for i in range(SHARD // CHUNK)
    ]
    small = [
        pltpu.make_async_copy(src, dst, small_sem.at[i])
        for i, (src, dst) in enumerate(
            (
                (q_hbm, queries.at[pl.ds(0, TOK)]),
                (cells_hbm, cells),
                (probes_hbm, probes),
                (codes_hbm, codes),
                (book_hbm, book),
                (locations_hbm, locations),
                (candidates_hbm, candidates),
                (lengths_hbm, lengths),
            )
        )
    ]
    for load in small + loads:
        load.start()

    barrier = pltpu.get_barrier_semaphore()
    partners = (
        [(cent_at(0, d), p) for d in (1, 2, 3)]
        + [(cent_at(d, 0), p) for d in (1, 2, 3)]
        + [(c, pass_at(d)) for d in range(1, 8)]
        + [(c, other)]
    )
    for partner in partners:
        pl.semaphore_signal(barrier, inc=1, device_id=partner, device_id_type=MESH)
    pl.semaphore_wait(barrier, len(partners))
    for load in small:
        load.wait()
    lane8 = lax.broadcasted_iota(jnp.int32, (8, 128), 1)
    sub8 = lax.broadcasted_iota(jnp.int32, (8, 128), 0)

    def send(src, dst, send_sem, recv_sem, target):
        pltpu.make_async_remote_copy(
            src_ref=src, dst_ref=dst, send_sem=send_sem, recv_sem=recv_sem, device_id=target, device_id_type=MESH
        ).start()

    def arrived(ref, sem):
        pltpu.make_async_remote_copy(
            src_ref=ref, dst_ref=ref, send_sem=sem, recv_sem=sem, device_id=(c, other), device_id_type=MESH
        ).wait_recv()

    def gone(ref, sem):
        pltpu.make_async_remote_copy(
            src_ref=ref, dst_ref=ref, send_sem=sem, recv_sem=sem, device_id=(c, other), device_id_type=MESH
        ).wait_send()

    for d in (1, 3, 2):
        send(queries.at[pl.ds(0, TOK)], queries.at[pl.ds(d * TOK, TOK)], qs.at[0], qr.at[0], (cent_at(0, d), p))
    for load in loads:
        load.wait()

    mine = [jnp.where(sub8 == r, c, -1) for r in range(8)]

    def pick(ids):
        parts = []
        for base in range(0, len(ids), 8):
            acc = jnp.zeros((8, DIM), F32)
            for r, i in enumerate(ids[base : base + 8]):
                pair = cent[(i & (SHARD - 1)) >> 4].astype(F32)
                ids_r = jnp.full((8, DIM), i, jnp.int32)
                half = jnp.where((ids_r & 8) != 0, pair[8:], pair[:8])
                row = jnp.take_along_axis(half, ids_r & 7, axis=0)
                acc = jnp.where(mine[r] == (ids_r >> SHIFT), row, acc)
            parts.append(acc)
        return jnp.concatenate(parts, axis=0).astype(BF16)

    def collect_first(i, carry):
        dx, dy = lax.rem(lax.div(i, 4) + 1, 4), lax.rem(i, 4)
        target = cent_at(4 - dy, 4 - dx)
        first_send[dx, dy] = pick([cells[target, min(j, PLEN - 1)] for j in range(32)])
        return carry

    def collect_second(i, carry):
        half, dy = lax.div(i, 4), lax.rem(i, 4)
        at = P_OWN - 8 + lax.div(cent_at(4 - dy, 4 - 2 * half - odd), 2)
        second_send[half, dy] = pick([cells[at, min(j, PLEN - 1)] for j in range(32)])
        return carry

    def collect_probed(d, carry):
        base = (cent_at(4 - lax.div(d, 4), 4 - lax.rem(d, 4)) * NP + p) * QD
        probed[pl.ds(pl.multiple_of(d * 16, 16), 16), :] = pick(
            [probes[k, base + q] for q in range(QD) for k in range(NPROBE)]
        )
        return carry

    lax.fori_loop(0, 12, collect_first, 0)
    for d in (1, 3, 2):
        send(first_send.at[d], first_recv.at[d], ws.at[0], wr.at[0], (cent_at(0, 4 - d), p))
    lax.fori_loop(0, 8, collect_second, 0)

    def send_second(half, d):
        send(second_send.at[half], second_recv.at[d], ws.at[1], wr.at[1], (cent_at(0, 4 - d), p))

    @pl.when(odd == 0)
    def _():
        send_second(1, 2)

    @pl.when(odd == 1)
    def _():
        send_second(0, 1)
        send_second(1, 3)

    arrived(queries.at[pl.ds(TOK, 3 * TOK)], qr.at[0])
    for d in (1, 3, 2):
        send(queries.at[pl.ds(0, TILE)], queries.at[pl.ds(d * TILE, TILE)], qs.at[d], qr.at[d], (cent_at(d, 0), p))
    lax.fori_loop(12, 16, collect_first, 0)
    lax.fori_loop(0, NC, collect_probed, 0)

    group8 = lane8 >> 5
    for base in range(0, CMAX, 8):
        found = jnp.full((8, 128), -1, jnp.int32)
        for q in range(QD):
            for r in range(8):
                at = locations[candidates[q, base + r]]
                found = jnp.where((sub8 == r) & (group8 == q), at, found)
            live = base + sub8 < lengths[q]
            found = jnp.where((group8 == q) & jnp.logical_not(live), -1, found)
        wanted[pl.ds(base, 8), :] = found

    def sum_rows():
        arrived(first_recv.at[pl.ds(1, 3)], wr.at[0])
        for dy in range(4):
            total = first_send[0, dy].astype(F32)
            for d in (1, 2, 3):
                total += first_recv[d, dy].astype(F32)
            column_send[dy] = total.astype(BF16)
        for dy in (1, 3, 2):
            send(column_send.at[dy], column_recv.at[dy], vs.at[0], vr.at[0], (cent_at(4 - dy, 0), p))

        @pl.when(odd == 0)
        def _():
            arrived(second_recv.at[pl.ds(1, 3)], wr.at[1])
            for dy in range(4):
                total = second_send[0, dy].astype(F32)
                for d in (1, 2, 3):
                    total += second_recv[d, dy].astype(F32)
                late_send[dy] = total.astype(BF16)
            for dy in (1, 3, 2):
                send(late_send.at[dy], late_recv.at[dy], vs.at[1], vr.at[1], (cent_at(4 - dy, 0), p))

    def decode(parts, at):
        rows = sum(parts[1:], parts[0])
        token = jnp.minimum(lax.broadcasted_iota(jnp.int32, (32, DIM), 0), PLEN - 1)
        shift = 2 * jnp.where(token >= 15, token - 15, token)
        words = codes[at]
        word = jnp.where(token >= 15, words[1:2, :], words[0:1, :])
        level = jnp.right_shift(word, shift) & 3
        residual = jnp.where(
            level < 2,
            jnp.where(level == 0, book[0:1, :], book[1:2, :]),
            jnp.where(level == 2, book[2:3, :], book[3:4, :]),
        )
        vector = rows + residual
        squares = jnp.sum(vector * vector, axis=-1, keepdims=True)
        return (vector * lax.rsqrt(squares + 1e-06)).astype(BF16)

    def build_passages():
        arrived(column_recv.at[pl.ds(1, 3)], vr.at[0])
        built = decode([column_send[0].astype(F32)] + [column_recv[d].astype(F32) for d in (1, 2, 3)], c)

        @pl.when(odd == 0)
        def _():
            arrived(late_recv.at[pl.ds(1, 3)], vr.at[1])
            passages[pl.ds(0, 32), :] = built
            passages[pl.ds(32, 32), :] = decode(
                [late_send[0].astype(F32)] + [late_recv[d].astype(F32) for d in (1, 2, 3)], second_of
            )
            for d in (4, 3, 5, 2, 6, 1, 7):
                send(passages.at[pl.ds(0, 64)], passages.at[pl.ds(d * 64, 64)], us.at[0], ur.at[0], (c, pass_at(d)))

        @pl.when(odd == 1)
        def _():
            passages[pl.ds(EVEN, 32), :] = built
            for d in (4, 3, 5, 2, 6, 1, 7):
                send(
                    passages.at[pl.ds(EVEN, 32)], passages.at[pl.ds(EVEN + d * 32, 32)], us.at[0], ur.at[0], (c, pass_at(d))
                )

    def relay_passages():
        @pl.when(odd == 0)
        def _():
            arrived(passages.at[pl.ds(64, EVEN - 64)], ur.at[0])
            send(passages.at[pl.ds(0, EVEN)], passages.at[pl.ds(0, EVEN)], us.at[1], ur.at[1], (c, other))

        @pl.when(odd == 1)
        def _():
            arrived(passages.at[pl.ds(EVEN + 32, 224)], ur.at[0])
            send(passages.at[pl.ds(EVEN, 256)], passages.at[pl.ds(EVEN, 256)], us.at[1], ur.at[1], (c, other))

    def products():
        @pl.when(odd == 0)
        def _():
            arrived(passages.at[pl.ds(EVEN, 256)], ur.at[1])

        @pl.when(odd == 1)
        def _():
            arrived(passages.at[pl.ds(0, EVEN)], ur.at[1])

        lane = lax.broadcasted_iota(jnp.int32, (TOK, 128), 1)
        token = lax.broadcasted_iota(jnp.int32, (TOK, 128), 0)
        weights = jnp.where(lane >> 5 == token >> 5, 1.0 / QT, 0.0).astype(BF16)
        diagonal = ((lane & 31) == (token & 31))[:32]

        def one_tile(t, carry):
            tile = queries[pl.ds(pl.multiple_of(t * TILE, TILE), TILE), :]
            dots = lax.dot_general(passages[...], tile, (((1,), (1,)), ((), ())), preferred_element_type=F32)
            most = jnp.max(dots.reshape(24, 32, TILE), axis=1)
            for i in range(TILE // TOK):
                part = jnp.concatenate([most[:, i * TOK : (i + 1) * TOK], jnp.zeros((8, TOK), F32)], axis=0)
                high = part.astype(BF16)
                low = (part - high.astype(F32)).astype(BF16)
                means = jnp.dot(high, weights, preferred_element_type=F32) + jnp.dot(
                    low, weights, preferred_element_type=F32
                )
                row = jnp.sum(jnp.where(diagonal, means, 0.0), axis=0, keepdims=True)
                result_send[t * (TILE // TOK) + i, pl.ds(5, 1), :] = row
            return carry

        lax.fori_loop(0, NC * TOK // TILE, one_tile, 0)

    def send_result(d):
        target = (cent_at(4 - d // 4, 4 - d % 4), p)
        send(result_send.at[d], result_recv.at[d], us.at[2], ur.at[2], target)

    def step(s, carry):
        t, i = lax.div(s, STEPS), lax.rem(s, STEPS)

        @pl.when(s == 2)
        def _():
            sum_rows()

        @pl.when(s == 4)
        def _():
            arrived(queries.at[pl.ds(TILE, TILE)], qr.at[1])

        @pl.when(s == 5)
        def _():
            build_passages()

        @pl.when(s == 8)
        def _():
            arrived(queries.at[pl.ds(2 * TILE, TILE)], qr.at[2])

        @pl.when(s == 10)
        def _():
            relay_passages()

        @pl.when(s == 12)
        def _():
            arrived(queries.at[pl.ds(3 * TILE, TILE)], qr.at[3])
            products()
            for d in range(1, 12):
                send_result(d)

        tile = queries[pl.ds(pl.multiple_of(t * TILE, TILE), TILE), :]
        rows = cent[pl.ds(i * (CHUNK // 16), CHUNK // 16)].reshape(CHUNK, DIM)
        dots = lax.dot_general(rows, tile, (((1,), (1,)), ((), ())), preferred_element_type=F32)
        most = jnp.max(dots.reshape(CHUNK // 8, 8, TILE), axis=0)
        most = jnp.maximum(most, jnp.where(i == 0, -jnp.inf, running[...]))
        running[...] = most

        @pl.when(i == STEPS - 1)
        def _():
            best = jnp.max(most, axis=0, keepdims=True)
            held = probed[pl.ds(pl.multiple_of(t * 64, 64), 64), :]
            found = lax.dot_general(held, tile, (((1,), (1,)), ((), ())), preferred_element_type=F32)
            for j in range(TILE // TOK):
                block = found[j * 16 : (j + 1) * 16, j * TOK : (j + 1) * TOK]
                pair = jnp.where(group8 == sub8 >> 2, block[:8], 0.0) + jnp.where(
                    group8 - 2 == sub8 >> 2, block[8:], 0.0
                )
                four = pair + pltpu.roll(pair, 4, 0)
                result_send[t * (TILE // TOK) + j, pl.ds(0, 5), :] = jnp.where(
                    sub8 < 4, four, jnp.broadcast_to(best[:, j * TOK : (j + 1) * TOK], (8, 128))
                )[:5]

        return carry

    running[...] = jnp.full((8, TILE), -jnp.inf, F32)
    lax.fori_loop(0, NC * TOK // TILE * STEPS, step, 0)
    for d in range(12, NC):
        send_result(d)

    place = lane8 & 31
    even = place < 16
    away = jnp.where(even, place >> 1, place - 16)
    base = lax.rem(z + 16 - away, 8) * (2 * P_OWN)
    base = jnp.where(place < 24, base, -1000)
    second = even & ((place & 1) == 1)
    nothing = [jnp.zeros((8, 128), F32) for _ in range(CMAX // 8)]

    def combine(cc, got, best, total, chosen):
        late = lax.rem(cc, 2)
        at = base + P_OWN * jnp.where(even, late, 1 - late) + jnp.where(second, P_OWN - 8 + lax.div(cc, 2), cc)
        scores = jnp.broadcast_to(got[5:6, :], (8, 128))
        chosen = [
            jnp.where(wanted[pl.ds(8 * g, 8), :] == at, scores, chosen[g]) for g in range(CMAX // 8)
        ]
        return jnp.maximum(best, got), total + got, chosen

    held = combine(c, result_send[0], jnp.full((8, 128), -jnp.inf, F32), jnp.zeros((8, 128), F32), nothing)
    gone(queries.at[pl.ds(0, 3 * TOK)], qs.at[0])
    for d in (1, 2, 3):
        gone(queries.at[pl.ds(0, TILE)], qs.at[d])
    gone(first_send.at[pl.ds(1, 3)], ws.at[0])
    gone(column_send.at[pl.ds(1, 3)], vs.at[0])

    @pl.when(odd == 0)
    def _():
        gone(second_send.at[1], ws.at[1])
        gone(late_send.at[pl.ds(1, 3)], vs.at[1])
        gone(passages.at[pl.ds(0, 7 * 64)], us.at[0])
        gone(passages.at[pl.ds(0, EVEN)], us.at[1])

    @pl.when(odd == 1)
    def _():
        gone(second_send, ws.at[1])
        gone(passages.at[pl.ds(EVEN, 7 * 32)], us.at[0])
        gone(passages.at[pl.ds(EVEN, 256)], us.at[1])

    gone(result_send.at[pl.ds(1, NC - 1)], us.at[2])
    arrived(result_recv.at[pl.ds(1, NC - 1)], ur.at[2])
    for d in range(1, NC):
        held = combine(cent_at(d // 4, d % 4), result_recv[d], *held)
    best, total, chosen = held
    chosen = jnp.concatenate(chosen, axis=0)
    ones = jnp.where(group8 == sub8, 1.0, 0.0).astype(BF16)
    scores = jnp.zeros((8, CMAX), F32)
    for _ in range(3):
        term = chosen.astype(BF16)
        scores += lax.dot_general(ones, term, (((1,), (1,)), ((), ())), preferred_element_type=F32)
        chosen = chosen - term.astype(F32)
    score_out[...] = scores[:QD]
    for q in range(QD):
        top_out[pl.ds(q, 1), :] = best[4:5, q * QT : (q + 1) * QT]
        probe_out[q] = total[:4, q * QT : (q + 1) * QT]


def deliver(top, probe, score, top_out, probe_out, score_out, sems):
    copies = [
        pltpu.make_async_copy(src, dst, sems.at[i])
        for i, (src, dst) in enumerate(((top, top_out), (probe, probe_out), (score, score_out)))
    ]
    for copy in copies:
        copy.start()
    for copy in copies:
        copy.wait()


def body(queries, probes, centroids, codebook, token_cells, codes, locations, candidates, lengths):
    vmem = pl.BlockSpec(memory_space=pltpu.VMEM)
    hbm = pl.BlockSpec(memory_space=pltpu.HBM)
    results = pl.pallas_call(
        kernel,
        out_shape=(
            jax.ShapeDtypeStruct((QD, QT), F32),
            jax.ShapeDtypeStruct((QD, NPROBE, QT), F32),
            jax.ShapeDtypeStruct((QD, CMAX), F32),
        ),
        in_specs=[hbm] * 9,
        out_specs=(vmem, vmem, vmem),
        scratch_shapes=[
            pltpu.SMEM((NPROBE, NC * NP * QD), jnp.int32),
            pltpu.SMEM((P_OWN, PLEN), jnp.int32),
            pltpu.VMEM((P_OWN, 2, DIM), jnp.int32),
            pltpu.VMEM((4, DIM), F32),
            pltpu.SMEM((NP * P_OWN,), jnp.int32),
            pltpu.SMEM((QD, CMAX), jnp.int32),
            pltpu.SMEM((QD,), jnp.int32),
            pltpu.VMEM((SHARD // 16, 16, DIM), BF16),
            pltpu.VMEM((NC * TOK, DIM), BF16),
            pltpu.VMEM((4, 4, 32, DIM), BF16),
            pltpu.VMEM((4, 4, 32, DIM), BF16),
            pltpu.VMEM((2, 4, 32, DIM), BF16),
            pltpu.VMEM((4, 4, 32, DIM), BF16),
            pltpu.VMEM((4, 32, DIM), BF16),
            pltpu.VMEM((4, 32, DIM), BF16),
            pltpu.VMEM((4, 32, DIM), BF16),
            pltpu.VMEM((4, 32, DIM), BF16),
            pltpu.VMEM((NC * 16, DIM), BF16),
            pltpu.VMEM((EVEN + 256, DIM), BF16),
            pltpu.VMEM((NC, 8, 128), F32),
            pltpu.VMEM((NC, 8, 128), F32),
            pltpu.VMEM((CMAX, 128), jnp.int32),
            pltpu.VMEM((8, TILE), F32),
            pltpu.SemaphoreType.DMA((STEPS,)),
            pltpu.SemaphoreType.DMA((8,)),
        ]
        + [pltpu.SemaphoreType.DMA((4,))] * 8,
        compiler_params=pltpu.CompilerParams(
            collective_id=0, has_side_effects=True, vmem_limit_bytes=60 << 20
        ),
        name="late_interaction",
    )(
        queries.reshape(TOK, DIM), probes.T, token_cells, codes, codebook, locations, candidates, lengths,
        centroids.reshape(SHARD // 16, 16, DIM),
    )
    top, probe, score = pl.pallas_call(
        deliver,
        out_shape=tuple(jax.ShapeDtypeStruct(r.shape, r.dtype) for r in results),
        in_specs=[hbm] * 3,
        out_specs=[hbm] * 3,
        scratch_shapes=[pltpu.SemaphoreType.DMA((3,))],
        name="deliver",
    )(*results)
    return top, jnp.transpose(probe, (0, 2, 1)), score


def solution(mesh):
    placed = (
        P(("cent", "pass"), None, None),
        P(),
        P("cent", None),
        P(),
        P("pass", None),
        P("pass", None, None),
        P(),
        P(("cent", "pass"), None),
        P(("cent", "pass")),
    )
    return jax.shard_map(
        body,
        mesh=mesh,
        in_specs=placed,
        out_specs=(
            P(("cent", "pass"), None),
            P(("cent", "pass"), None, None),
            P(("cent", "pass"), None),
        ),
        check_vma=False,
    )
```

```python
import jax
import jax.numpy as jnp
from jax import lax
from jax.experimental import pallas as pl
from jax.experimental.pallas import tpu as pltpu
from jax.sharding import PartitionSpec as P

MESH = pl.DeviceIdType.MESH
DIM = 128
QT = 32
NPROBE = 4
PLEN = 30
P_OWN = 24
CMAX = 40
NC = 16
NP = 16
QD = 4
TOK = QD * QT
SHARD = 16384
SHIFT = 14
CHUNK = 4096
TILE = 512
STEPS = SHARD // CHUNK
EVEN = 8 * 64
F32 = jnp.float32
BF16 = jnp.bfloat16


def kernel(
    q_hbm, probes_hbm, cells_hbm, codes_hbm, book_hbm, locations_hbm, candidates_hbm, lengths_hbm, cent_hbm,
    top_out, probe_out, score_out,
    probes, cells, codes, book, locations, candidates, lengths,
    cent, queries, first_send, first_recv, second_send, second_recv, column_send, column_recv, late_send, late_recv,
    probed, passages, result_send, result_recv, wanted, running,
    load_sem, small_sem, plane_here, line_here, qs, qr, ws, wr, vs, vr, us, ur,
):
    c = lax.axis_index("cent")
    p = lax.axis_index("pass")
    y, x = lax.div(c, 4), lax.rem(c, 4)
    z, core = lax.div(p, 2), lax.rem(p, 2)
    odd = lax.rem(c + p, 2)
    second_of = P_OWN - 8 + lax.div(c, 2)

    def cent_at(dy, dx):
        return lax.rem(y + dy, 4) * 4 + lax.rem(x + dx, 4)

    def pass_at(dz):
        return lax.rem(z + dz, 8) * 2 + core

    other = z * 2 + 1 - core

    loads = [
        pltpu.make_async_copy(
            cent_hbm.at[pl.ds(i * CHUNK // 16, CHUNK // 16)], cent.at[pl.ds(i * CHUNK // 16, CHUNK // 16)], load_sem.at[i]
        )
        for i in range(SHARD // CHUNK)
    ]
    small = [
        pltpu.make_async_copy(src, dst, small_sem.at[i])
        for i, (src, dst) in enumerate(
            (
                (q_hbm, queries.at[pl.ds(0, TOK)]),
                (cells_hbm, cells),
                (probes_hbm, probes),
                (codes_hbm, codes),
                (book_hbm, book),
                (locations_hbm, locations),
                (candidates_hbm, candidates),
                (lengths_hbm, lengths),
            )
        )
    ]
    for load in small + loads:
        load.start()

    barrier = pltpu.get_barrier_semaphore()
    for d in (1, 2, 3):
        for there in (cent_at(0, d), cent_at(d, 0)):
            pl.semaphore_signal(barrier, inc=1, device_id=(there, z * 2), device_id_type=MESH)
    for d in range(1, 8):
        pl.semaphore_signal(
            barrier, inc=1, device_id=(c, lax.rem(z + d, 8) * 2 + 1), device_id_type=MESH
        )

    @pl.when(core == 1)
    def _():
        pl.semaphore_signal(barrier, inc=1, device_id=(c, other), device_id_type=MESH)
        pl.semaphore_wait(plane_here, 1)

    @pl.when(core == 0)
    def _():
        pl.semaphore_wait(barrier, 13)
        pl.semaphore_signal(plane_here, inc=1, device_id=(c, other), device_id_type=MESH)

    for load in small:
        load.wait()
    lane8 = lax.broadcasted_iota(jnp.int32, (8, 128), 1)
    sub8 = lax.broadcasted_iota(jnp.int32, (8, 128), 0)

    def send(src, dst, send_sem, recv_sem, target):
        pltpu.make_async_remote_copy(
            src_ref=src, dst_ref=dst, send_sem=send_sem, recv_sem=recv_sem, device_id=target, device_id_type=MESH
        ).start()

    def arrived(ref, sem):
        pltpu.make_async_remote_copy(
            src_ref=ref, dst_ref=ref, send_sem=sem, recv_sem=sem, device_id=(c, other), device_id_type=MESH
        ).wait_recv()

    def gone(ref, sem):
        pltpu.make_async_remote_copy(
            src_ref=ref, dst_ref=ref, send_sem=sem, recv_sem=sem, device_id=(c, other), device_id_type=MESH
        ).wait_send()

    for d in (1, 3, 2):
        send(queries.at[pl.ds(0, TOK)], queries.at[pl.ds(d * TOK, TOK)], qs.at[0], qr.at[0], (cent_at(0, d), p))
    for load in loads:
        load.wait()

    mine = [jnp.where(sub8 == r, c, -1) for r in range(8)]

    def pick(ids):
        parts = []
        for base in range(0, len(ids), 8):
            acc = jnp.zeros((8, DIM), F32)
            for r, i in enumerate(ids[base : base + 8]):
                pair = cent[(i & (SHARD - 1)) >> 4].astype(F32)
                ids_r = jnp.full((8, DIM), i, jnp.int32)
                half = jnp.where((ids_r & 8) != 0, pair[8:], pair[:8])
                row = jnp.take_along_axis(half, ids_r & 7, axis=0)
                acc = jnp.where(mine[r] == (ids_r >> SHIFT), row, acc)
            parts.append(acc)
        return jnp.concatenate(parts, axis=0).astype(BF16)

    def collect_first(i, carry):
        dx, dy = lax.rem(lax.div(i, 4) + 1, 4), lax.rem(i, 4)
        target = cent_at(4 - dy, 4 - dx)
        first_send[dx, dy] = pick([cells[target, min(j, PLEN - 1)] for j in range(32)])
        return carry

    def collect_second(i, carry):
        half, dy = lax.div(i, 4), lax.rem(i, 4)
        at = P_OWN - 8 + lax.div(cent_at(4 - dy, 4 - 2 * half - odd), 2)
        second_send[half, dy] = pick([cells[at, min(j, PLEN - 1)] for j in range(32)])
        return carry

    def collect_probed(d, carry):
        base = (cent_at(4 - lax.div(d, 4), 4 - lax.rem(d, 4)) * NP + p) * QD
        probed[pl.ds(pl.multiple_of(d * 16, 16), 16), :] = pick(
            [probes[k, base + q] for q in range(QD) for k in range(NPROBE)]
        )
        return carry

    lax.fori_loop(0, 12, collect_first, 0)
    for d in (1, 3, 2):
        send(first_send.at[d], first_recv.at[d], ws.at[0], wr.at[0], (cent_at(0, 4 - d), p))
    lax.fori_loop(0, 8, collect_second, 0)

    def send_second(half, d):
        send(second_send.at[half], second_recv.at[d], ws.at[1], wr.at[1], (cent_at(0, 4 - d), p))

    @pl.when(odd == 0)
    def _():
        send_second(1, 2)

    @pl.when(odd == 1)
    def _():
        send_second(0, 1)
        send_second(1, 3)

    arrived(queries.at[pl.ds(TOK, 3 * TOK)], qr.at[0])
    for d in (1, 3, 2):
        send(queries.at[pl.ds(0, TILE)], queries.at[pl.ds(d * TILE, TILE)], qs.at[d], qr.at[d], (cent_at(d, 0), p))
    lax.fori_loop(12, 16, collect_first, 0)
    lax.fori_loop(0, NC, collect_probed, 0)

    group8 = lane8 >> 5
    for base in range(0, CMAX, 8):
        found = jnp.full((8, 128), -1, jnp.int32)
        for q in range(QD):
            for r in range(8):
                at = locations[candidates[q, base + r]]
                found = jnp.where((sub8 == r) & (group8 == q), at, found)
            live = base + sub8 < lengths[q]
            found = jnp.where((group8 == q) & jnp.logical_not(live), -1, found)
        wanted[pl.ds(base, 8), :] = found

    def sum_rows():
        arrived(first_recv.at[pl.ds(1, 3)], wr.at[0])
        for dy in range(4):
            total = first_send[0, dy].astype(F32)
            for d in (1, 2, 3):
                total += first_recv[d, dy].astype(F32)
            column_send[dy] = total.astype(BF16)
        for dy in (1, 3, 2):
            send(column_send.at[dy], column_recv.at[dy], vs.at[0], vr.at[0], (cent_at(4 - dy, 0), p))

        @pl.when(odd == 0)
        def _():
            arrived(second_recv.at[pl.ds(1, 3)], wr.at[1])
            for dy in range(4):
                total = second_send[0, dy].astype(F32)
                for d in (1, 2, 3):
                    total += second_recv[d, dy].astype(F32)
                late_send[dy] = total.astype(BF16)
            for dy in (1, 3, 2):
                send(late_send.at[dy], late_recv.at[dy], vs.at[1], vr.at[1], (cent_at(4 - dy, 0), p))

    def decode(parts, at):
        rows = sum(parts[1:], parts[0])
        token = jnp.minimum(lax.broadcasted_iota(jnp.int32, (32, DIM), 0), PLEN - 1)
        shift = 2 * jnp.where(token >= 15, token - 15, token)
        words = codes[at]
        word = jnp.where(token >= 15, words[1:2, :], words[0:1, :])
        level = jnp.right_shift(word, shift) & 3
        residual = jnp.where(
            level < 2,
            jnp.where(level == 0, book[0:1, :], book[1:2, :]),
            jnp.where(level == 2, book[2:3, :], book[3:4, :]),
        )
        vector = rows + residual
        squares = jnp.sum(vector * vector, axis=-1, keepdims=True)
        return (vector * lax.rsqrt(squares + 1e-06)).astype(BF16)

    def await_line():
        @pl.when(core == 1)
        def _():
            pl.semaphore_wait(barrier, 14)
            pl.semaphore_signal(line_here, inc=1, device_id=(c, other), device_id_type=MESH)

        @pl.when(core == 0)
        def _():
            pl.semaphore_wait(line_here, 1)

    def build_passages():
        arrived(column_recv.at[pl.ds(1, 3)], vr.at[0])
        built = decode([column_send[0].astype(F32)] + [column_recv[d].astype(F32) for d in (1, 2, 3)], c)

        @pl.when(odd == 0)
        def _():
            arrived(late_recv.at[pl.ds(1, 3)], vr.at[1])
            passages[pl.ds(0, 32), :] = built
            passages[pl.ds(32, 32), :] = decode(
                [late_send[0].astype(F32)] + [late_recv[d].astype(F32) for d in (1, 2, 3)], second_of
            )
            for d in (4, 3, 5, 2, 6, 1, 7):
                send(passages.at[pl.ds(0, 64)], passages.at[pl.ds(d * 64, 64)], us.at[0], ur.at[0], (c, pass_at(d)))

        @pl.when(odd == 1)
        def _():
            passages[pl.ds(EVEN, 32), :] = built
            for d in (4, 3, 5, 2, 6, 1, 7):
                send(
                    passages.at[pl.ds(EVEN, 32)], passages.at[pl.ds(EVEN + d * 32, 32)], us.at[0], ur.at[0], (c, pass_at(d))
                )

    def relay_passages():
        @pl.when(odd == 0)
        def _():
            arrived(passages.at[pl.ds(64, EVEN - 64)], ur.at[0])
            send(passages.at[pl.ds(0, EVEN)], passages.at[pl.ds(0, EVEN)], us.at[1], ur.at[1], (c, other))

        @pl.when(odd == 1)
        def _():
            arrived(passages.at[pl.ds(EVEN + 32, 224)], ur.at[0])
            send(passages.at[pl.ds(EVEN, 256)], passages.at[pl.ds(EVEN, 256)], us.at[1], ur.at[1], (c, other))

    def products():
        @pl.when(odd == 0)
        def _():
            arrived(passages.at[pl.ds(EVEN, 256)], ur.at[1])

        @pl.when(odd == 1)
        def _():
            arrived(passages.at[pl.ds(0, EVEN)], ur.at[1])

        lane = lax.broadcasted_iota(jnp.int32, (TOK, 128), 1)
        token = lax.broadcasted_iota(jnp.int32, (TOK, 128), 0)
        weights = jnp.where(lane >> 5 == token >> 5, 1.0 / QT, 0.0).astype(BF16)
        diagonal = ((lane & 31) == (token & 31))[:32]

        def one_tile(t, carry):
            tile = queries[pl.ds(pl.multiple_of(t * TILE, TILE), TILE), :]
            dots = lax.dot_general(passages[...], tile, (((1,), (1,)), ((), ())), preferred_element_type=F32)
            most = jnp.max(dots.reshape(24, 32, TILE), axis=1)
            for i in range(TILE // TOK):
                part = jnp.concatenate([most[:, i * TOK : (i + 1) * TOK], jnp.zeros((8, TOK), F32)], axis=0)
                high = part.astype(BF16)
                low = (part - high.astype(F32)).astype(BF16)
                means = jnp.dot(high, weights, preferred_element_type=F32) + jnp.dot(
                    low, weights, preferred_element_type=F32
                )
                row = jnp.sum(jnp.where(diagonal, means, 0.0), axis=0, keepdims=True)
                result_send[t * (TILE // TOK) + i, pl.ds(5, 1), :] = row
            return carry

        lax.fori_loop(0, NC * TOK // TILE, one_tile, 0)

    def send_result(d):
        target = (cent_at(4 - d // 4, 4 - d % 4), p)
        send(result_send.at[d], result_recv.at[d], us.at[2], ur.at[2], target)

    def step(s, carry):
        t, i = lax.div(s, STEPS), lax.rem(s, STEPS)

        @pl.when(s == 2)
        def _():
            sum_rows()

        @pl.when(s == 4)
        def _():
            arrived(queries.at[pl.ds(TILE, TILE)], qr.at[1])

        @pl.when(s == 5)
        def _():
            await_line()
            build_passages()

        @pl.when(s == 8)
        def _():
            arrived(queries.at[pl.ds(2 * TILE, TILE)], qr.at[2])

        @pl.when(s == 13)
        def _():
            relay_passages()

        @pl.when(s == 12)
        def _():
            arrived(queries.at[pl.ds(3 * TILE, TILE)], qr.at[3])

        @pl.when(s == 15)
        def _():
            products()
            for d in range(1, 12):
                send_result(d)

        tile = queries[pl.ds(pl.multiple_of(t * TILE, TILE), TILE), :]
        rows = cent[pl.ds(i * (CHUNK // 16), CHUNK // 16)].reshape(CHUNK, DIM)
        dots = lax.dot_general(rows, tile, (((1,), (1,)), ((), ())), preferred_element_type=F32)
        most = jnp.max(dots.reshape(CHUNK // 8, 8, TILE), axis=0)
        most = jnp.maximum(most, jnp.where(i == 0, -jnp.inf, running[...]))
        running[...] = most

        @pl.when(i == STEPS - 1)
        def _():
            best = jnp.max(most, axis=0, keepdims=True)
            held = probed[pl.ds(pl.multiple_of(t * 64, 64), 64), :]
            found = lax.dot_general(held, tile, (((1,), (1,)), ((), ())), preferred_element_type=F32)
            for j in range(TILE // TOK):
                block = found[j * 16 : (j + 1) * 16, j * TOK : (j + 1) * TOK]
                pair = jnp.where(group8 == sub8 >> 2, block[:8], 0.0) + jnp.where(
                    group8 - 2 == sub8 >> 2, block[8:], 0.0
                )
                four = pair + pltpu.roll(pair, 4, 0)
                result_send[t * (TILE // TOK) + j, pl.ds(0, 5), :] = jnp.where(
                    sub8 < 4, four, jnp.broadcast_to(best[:, j * TOK : (j + 1) * TOK], (8, 128))
                )[:5]

        return carry

    running[...] = jnp.full((8, TILE), -jnp.inf, F32)
    lax.fori_loop(0, NC * TOK // TILE * STEPS, step, 0)
    for d in range(12, NC):
        send_result(d)

    place = lane8 & 31
    even = place < 16
    away = jnp.where(even, place >> 1, place - 16)
    base = lax.rem(z + 16 - away, 8) * (2 * P_OWN)
    base = jnp.where(place < 24, base, -1000)
    second = even & ((place & 1) == 1)
    nothing = [jnp.zeros((8, 128), F32) for _ in range(CMAX // 8)]

    def combine(cc, got, best, total, chosen):
        late = lax.rem(cc, 2)
        at = base + P_OWN * jnp.where(even, late, 1 - late) + jnp.where(second, P_OWN - 8 + lax.div(cc, 2), cc)
        scores = jnp.broadcast_to(got[5:6, :], (8, 128))
        chosen = [
            jnp.where(wanted[pl.ds(8 * g, 8), :] == at, scores, chosen[g]) for g in range(CMAX // 8)
        ]
        return jnp.maximum(best, got), total + got, chosen

    held = combine(c, result_send[0], jnp.full((8, 128), -jnp.inf, F32), jnp.zeros((8, 128), F32), nothing)
    gone(queries.at[pl.ds(0, 3 * TOK)], qs.at[0])
    for d in (1, 2, 3):
        gone(queries.at[pl.ds(0, TILE)], qs.at[d])
    gone(first_send.at[pl.ds(1, 3)], ws.at[0])
    gone(column_send.at[pl.ds(1, 3)], vs.at[0])

    @pl.when(odd == 0)
    def _():
        gone(second_send.at[1], ws.at[1])
        gone(late_send.at[pl.ds(1, 3)], vs.at[1])
        gone(passages.at[pl.ds(0, 7 * 64)], us.at[0])
        gone(passages.at[pl.ds(0, EVEN)], us.at[1])

    @pl.when(odd == 1)
    def _():
        gone(second_send, ws.at[1])
        gone(passages.at[pl.ds(EVEN, 7 * 32)], us.at[0])
        gone(passages.at[pl.ds(EVEN, 256)], us.at[1])

    gone(result_send.at[pl.ds(1, NC - 1)], us.at[2])
    arrived(result_recv.at[pl.ds(1, NC - 1)], ur.at[2])
    for d in range(1, NC):
        held = combine(cent_at(d // 4, d % 4), result_recv[d], *held)
    best, total, chosen = held
    chosen = jnp.concatenate(chosen, axis=0)
    ones = jnp.where(group8 == sub8, 1.0, 0.0).astype(BF16)
    scores = jnp.zeros((8, CMAX), F32)
    for _ in range(3):
        term = chosen.astype(BF16)
        scores += lax.dot_general(ones, term, (((1,), (1,)), ((), ())), preferred_element_type=F32)
        chosen = chosen - term.astype(F32)
    score_out[...] = scores[:QD]
    for q in range(QD):
        top_out[pl.ds(q, 1), :] = best[4:5, q * QT : (q + 1) * QT]
        probe_out[q] = total[:4, q * QT : (q + 1) * QT]


def deliver(top, probe, score, top_out, probe_out, score_out, sems):
    copies = [
        pltpu.make_async_copy(src, dst, sems.at[i])
        for i, (src, dst) in enumerate(((top, top_out), (probe, probe_out), (score, score_out)))
    ]
    for copy in copies:
        copy.start()
    for copy in copies:
        copy.wait()


def body(queries, probes, centroids, codebook, token_cells, codes, locations, candidates, lengths):
    vmem = pl.BlockSpec(memory_space=pltpu.VMEM)
    hbm = pl.BlockSpec(memory_space=pltpu.HBM)
    results = pl.pallas_call(
        kernel,
        out_shape=(
            jax.ShapeDtypeStruct((QD, QT), F32),
            jax.ShapeDtypeStruct((QD, NPROBE, QT), F32),
            jax.ShapeDtypeStruct((QD, CMAX), F32),
        ),
        in_specs=[hbm] * 9,
        out_specs=(vmem, vmem, vmem),
        scratch_shapes=[
            pltpu.SMEM((NPROBE, NC * NP * QD), jnp.int32),
            pltpu.SMEM((P_OWN, PLEN), jnp.int32),
            pltpu.VMEM((P_OWN, 2, DIM), jnp.int32),
            pltpu.VMEM((4, DIM), F32),
            pltpu.SMEM((NP * P_OWN,), jnp.int32),
            pltpu.SMEM((QD, CMAX), jnp.int32),
            pltpu.SMEM((QD,), jnp.int32),
            pltpu.VMEM((SHARD // 16, 16, DIM), BF16),
            pltpu.VMEM((NC * TOK, DIM), BF16),
            pltpu.VMEM((4, 4, 32, DIM), BF16),
            pltpu.VMEM((4, 4, 32, DIM), BF16),
            pltpu.VMEM((2, 4, 32, DIM), BF16),
            pltpu.VMEM((4, 4, 32, DIM), BF16),
            pltpu.VMEM((4, 32, DIM), BF16),
            pltpu.VMEM((4, 32, DIM), BF16),
            pltpu.VMEM((4, 32, DIM), BF16),
            pltpu.VMEM((4, 32, DIM), BF16),
            pltpu.VMEM((NC * 16, DIM), BF16),
            pltpu.VMEM((EVEN + 256, DIM), BF16),
            pltpu.VMEM((NC, 8, 128), F32),
            pltpu.VMEM((NC, 8, 128), F32),
            pltpu.VMEM((CMAX, 128), jnp.int32),
            pltpu.VMEM((8, TILE), F32),
            pltpu.SemaphoreType.DMA((STEPS,)),
            pltpu.SemaphoreType.DMA((8,)),
            pltpu.SemaphoreType.REGULAR,
            pltpu.SemaphoreType.REGULAR,
        ]
        + [pltpu.SemaphoreType.DMA((4,))] * 8,
        compiler_params=pltpu.CompilerParams(
            collective_id=0, has_side_effects=True, vmem_limit_bytes=60 << 20
        ),
        name="late_interaction",
    )(
        queries.reshape(TOK, DIM), probes.T, token_cells, codes, codebook, locations, candidates, lengths,
        centroids.reshape(SHARD // 16, 16, DIM),
    )
    top, probe, score = pl.pallas_call(
        deliver,
        out_shape=tuple(jax.ShapeDtypeStruct(r.shape, r.dtype) for r in results),
        in_specs=[hbm] * 3,
        out_specs=[hbm] * 3,
        scratch_shapes=[pltpu.SemaphoreType.DMA((3,))],
        name="deliver",
    )(*results)
    return top, jnp.transpose(probe, (0, 2, 1)), score


def solution(mesh):
    placed = (
        P(("cent", "pass"), None, None),
        P(),
        P("cent", None),
        P(),
        P("pass", None),
        P("pass", None, None),
        P(),
        P(("cent", "pass"), None),
        P(("cent", "pass")),
    )
    return jax.shard_map(
        body,
        mesh=mesh,
        in_specs=placed,
        out_specs=(
            P(("cent", "pass"), None),
            P(("cent", "pass"), None, None),
            P(("cent", "pass"), None),
        ),
        check_vma=False,
    )
```

```python
import jax
import jax.numpy as jnp
from jax import lax
from jax.experimental import pallas as pl
from jax.experimental.pallas import tpu as pltpu
from jax.sharding import PartitionSpec as P

MESH = pl.DeviceIdType.MESH
DIM = 128
QT = 32
NPROBE = 4
PLEN = 30
P_OWN = 24
CMAX = 40
NC = 16
NP = 16
QD = 4
TOK = QD * QT
SHARD = 16384
SHIFT = 14
CHUNK = 4096
TILE = 512
WIDE = 1024
STEPS = SHARD // CHUNK
SUM_AT = 3
BUILD_AT = 6
PRODUCTS_AT = 14
EVEN = 8 * 64
F32 = jnp.float32
BF16 = jnp.bfloat16


def kernel(
    q_hbm, probes_hbm, cells_hbm, codes_hbm, book_hbm, locations_hbm, candidates_hbm, lengths_hbm, cent_hbm,
    out,
    probes, cells, codes, book, locations, candidates, lengths,
    cent, queries, first_send, first_recv, second_send, second_recv, column_send, column_recv, late_send, late_recv,
    probed, passages, result_send, result_recv, wanted, running,
    load_sem, small_sem, plane_here, line_here, qs, qr, ws, wr, vs, vr, us, ur,
):
    c = lax.axis_index("cent")
    p = lax.axis_index("pass")
    y, x = lax.div(c, 4), lax.rem(c, 4)
    z, core = lax.div(p, 2), lax.rem(p, 2)
    odd = lax.rem(c + p, 2)
    second_of = P_OWN - 8 + lax.div(c, 2)

    def cent_at(dy, dx):
        return lax.rem(y + dy, 4) * 4 + lax.rem(x + dx, 4)

    def pass_at(dz):
        return lax.rem(z + dz, 8) * 2 + core

    other = z * 2 + 1 - core

    loads = [
        pltpu.make_async_copy(
            cent_hbm.at[pl.ds(i * CHUNK // 16, CHUNK // 16)], cent.at[pl.ds(i * CHUNK // 16, CHUNK // 16)], load_sem.at[i]
        )
        for i in range(SHARD // CHUNK)
    ]
    small = [
        pltpu.make_async_copy(src, dst, small_sem.at[i])
        for i, (src, dst) in enumerate(
            (
                (q_hbm, queries.at[pl.ds(0, TOK)]),
                (cells_hbm, cells),
                (probes_hbm, probes),
                (codes_hbm, codes),
                (book_hbm, book),
                (locations_hbm, locations),
                (candidates_hbm, candidates),
                (lengths_hbm, lengths),
            )
        )
    ]
    for load in small + loads:
        load.start()

    barrier = pltpu.get_barrier_semaphore()
    for d in (2, 1, 3):
        for there in (cent_at(0, d), cent_at(d, 0)):
            pl.semaphore_signal(barrier, inc=1, device_id=(there, z * 2), device_id_type=MESH)
    for d in range(1, 8):
        pl.semaphore_signal(
            barrier, inc=1, device_id=(c, lax.rem(z + d, 8) * 2 + 1), device_id_type=MESH
        )

    @pl.when(core == 1)
    def _():
        pl.semaphore_signal(barrier, inc=1, device_id=(c, other), device_id_type=MESH)
        pl.semaphore_wait(plane_here, 1)

    @pl.when(core == 0)
    def _():
        pl.semaphore_wait(barrier, 13)
        pl.semaphore_signal(plane_here, inc=1, device_id=(c, other), device_id_type=MESH)

    small[0].wait()
    lane8 = lax.broadcasted_iota(jnp.int32, (8, 128), 1)
    sub8 = lax.broadcasted_iota(jnp.int32, (8, 128), 0)

    def send(src, dst, send_sem, recv_sem, target):
        pltpu.make_async_remote_copy(
            src_ref=src, dst_ref=dst, send_sem=send_sem, recv_sem=recv_sem, device_id=target, device_id_type=MESH
        ).start()

    def arrived(ref, sem):
        pltpu.make_async_remote_copy(
            src_ref=ref, dst_ref=ref, send_sem=sem, recv_sem=sem, device_id=(c, other), device_id_type=MESH
        ).wait_recv()

    def gone(ref, sem):
        pltpu.make_async_remote_copy(
            src_ref=ref, dst_ref=ref, send_sem=sem, recv_sem=sem, device_id=(c, other), device_id_type=MESH
        ).wait_send()

    for d in (1, 3, 2):
        send(queries.at[pl.ds(0, TOK)], queries.at[pl.ds(d * TOK, TOK)], qs.at[0], qr.at[0], (cent_at(0, d), p))
    for load in small[1:] + loads:
        load.wait()

    mine = [jnp.where(sub8 == r, c, -1) for r in range(8)]

    def pick(ids):
        parts = []
        for base in range(0, len(ids), 8):
            acc = jnp.zeros((8, DIM), F32)
            for r, i in enumerate(ids[base : base + 8]):
                pair = cent[(i & (SHARD - 1)) >> 4].astype(F32)
                ids_r = jnp.full((8, DIM), i, jnp.int32)
                half = jnp.where((ids_r & 8) != 0, pair[8:], pair[:8])
                row = jnp.take_along_axis(half, ids_r & 7, axis=0)
                acc = jnp.where(mine[r] == (ids_r >> SHIFT), row, acc)
            parts.append(acc)
        return jnp.concatenate(parts, axis=0).astype(BF16)

    def collect_first(i, carry):
        dx, dy = lax.rem(lax.div(i, 4) + 1, 4), lax.rem(i, 4)
        target = cent_at(4 - dy, 4 - dx)
        first_send[dx, dy] = pick([cells[target, min(j, PLEN - 1)] for j in range(32)])
        return carry

    def collect_second(i, carry):
        half, dy = lax.div(i, 4), lax.rem(i, 4)
        at = P_OWN - 8 + lax.div(cent_at(4 - dy, 4 - 2 * half - odd), 2)
        second_send[half, dy] = pick([cells[at, min(j, PLEN - 1)] for j in range(32)])
        return carry

    def collect_probed(d):
        base = (cent_at(4 - lax.div(d, 4), 4 - lax.rem(d, 4)) * NP + p) * QD
        probed[pl.ds(pl.multiple_of(d * 16, 16), 16), :] = pick(
            [probes[k, base + q] for q in range(QD) for k in range(NPROBE)]
        )

    lax.fori_loop(0, 12, collect_first, 0)
    for d in (1, 3, 2):
        send(first_send.at[d], first_recv.at[d], ws.at[0], wr.at[0], (cent_at(0, 4 - d), p))
    lax.fori_loop(0, 8, collect_second, 0)

    def send_second(half, d):
        send(second_send.at[half], second_recv.at[d], ws.at[1], wr.at[1], (cent_at(0, 4 - d), p))

    @pl.when(odd == 0)
    def _():
        send_second(1, 2)

    @pl.when(odd == 1)
    def _():
        send_second(0, 1)
        send_second(1, 3)

    arrived(queries.at[pl.ds(TOK, 3 * TOK)], qr.at[0])
    for d in (1, 3, 2):
        send(queries.at[pl.ds(0, TILE)], queries.at[pl.ds(d * TILE, TILE)], qs.at[d], qr.at[d], (cent_at(d, 0), p))

    group8 = lane8 >> 5
    for base in range(0, CMAX, 8):
        found = jnp.full((8, 128), -1, jnp.int32)
        for q in range(QD):
            for r in range(8):
                at = locations[candidates[q, base + r]]
                found = jnp.where((sub8 == r) & (group8 == q), at, found)
            live = base + sub8 < lengths[q]
            found = jnp.where((group8 == q) & jnp.logical_not(live), -1, found)
        wanted[pl.ds(base, 8), :] = found

    def sum_rows():
        arrived(first_recv.at[pl.ds(1, 3)], wr.at[0])
        for dy in range(4):
            total = first_send[0, dy].astype(F32)
            for d in (1, 2, 3):
                total += first_recv[d, dy].astype(F32)
            column_send[dy] = total.astype(BF16)
        for dy in (1, 3, 2):
            send(column_send.at[dy], column_recv.at[dy], vs.at[0], vr.at[0], (cent_at(4 - dy, 0), p))

        @pl.when(odd == 0)
        def _():
            arrived(second_recv.at[pl.ds(1, 3)], wr.at[1])
            for dy in range(4):
                total = second_send[0, dy].astype(F32)
                for d in (1, 2, 3):
                    total += second_recv[d, dy].astype(F32)
                late_send[dy] = total.astype(BF16)
            for dy in (1, 3, 2):
                send(late_send.at[dy], late_recv.at[dy], vs.at[1], vr.at[1], (cent_at(4 - dy, 0), p))

    def decode(parts, at):
        rows = sum(parts[1:], parts[0])
        token = jnp.minimum(lax.broadcasted_iota(jnp.int32, (32, DIM), 0), PLEN - 1)
        shift = 2 * jnp.where(token >= 15, token - 15, token)
        words = codes[at]
        word = jnp.where(token >= 15, words[1:2, :], words[0:1, :])
        level = jnp.right_shift(word, shift) & 3
        residual = jnp.where(
            level < 2,
            jnp.where(level == 0, book[0:1, :], book[1:2, :]),
            jnp.where(level == 2, book[2:3, :], book[3:4, :]),
        )
        vector = rows + residual
        squares = jnp.sum(vector * vector, axis=-1, keepdims=True)
        return (vector * lax.rsqrt(squares + 1e-06)).astype(BF16)

    def await_line():
        @pl.when(core == 1)
        def _():
            pl.semaphore_wait(barrier, 14)
            pl.semaphore_signal(line_here, inc=1, device_id=(c, other), device_id_type=MESH)

        @pl.when(core == 0)
        def _():
            pl.semaphore_wait(line_here, 1)

    def send_passages(start, size, d, near):
        i = 0 if near else 1
        there = pass_at(d) if near else lax.rem(z + d, 8) * 2 + 1 - core
        send(
            passages.at[pl.ds(start, size)], passages.at[pl.ds(start + d * size, size)], us.at[i], ur.at[i], (c, there)
        )

    def build_passages():
        arrived(column_recv.at[pl.ds(1, 3)], vr.at[0])
        built = decode([column_send[0].astype(F32)] + [column_recv[d].astype(F32) for d in (1, 2, 3)], c)

        @pl.when(odd == 0)
        def _():
            arrived(late_recv.at[pl.ds(1, 3)], vr.at[1])
            passages[pl.ds(0, 32), :] = built
            passages[pl.ds(32, 32), :] = decode(
                [late_send[0].astype(F32)] + [late_recv[d].astype(F32) for d in (1, 2, 3)], second_of
            )
            for d in (4, 3, 5, 2, 6, 1, 7, 0):
                for near in ((True, False) if d else (False,)):
                    send_passages(0, 64, d, near)

        @pl.when(odd == 1)
        def _():
            passages[pl.ds(EVEN, 32), :] = built
            for d in (4, 3, 5, 2, 6, 1, 7, 0):
                for near in ((True, False) if d else (False,)):
                    send_passages(EVEN, 32, d, near)

    def products():
        @pl.when(odd == 0)
        def _():
            arrived(passages.at[pl.ds(64, EVEN - 64)], ur.at[0])
            arrived(passages.at[pl.ds(EVEN, 256)], ur.at[1])

        @pl.when(odd == 1)
        def _():
            arrived(passages.at[pl.ds(EVEN + 32, 224)], ur.at[0])
            arrived(passages.at[pl.ds(0, EVEN)], ur.at[1])

        lane = lax.broadcasted_iota(jnp.int32, (TOK, 128), 1)
        token = lax.broadcasted_iota(jnp.int32, (TOK, 128), 0)
        weights = jnp.where(lane >> 5 == token >> 5, 1.0 / QT, 0.0).astype(BF16)
        diagonal = ((lane & 31) == (token & 31))[:32]

        def one_tile(t, carry):
            tile = queries[pl.ds(pl.multiple_of(t * WIDE, WIDE), WIDE), :]
            dots = lax.dot_general(passages[...], tile, (((1,), (1,)), ((), ())), preferred_element_type=F32)
            most = jnp.max(dots.reshape(24, 32, WIDE), axis=1)
            for i in range(WIDE // TOK):
                part = jnp.concatenate([most[:, i * TOK : (i + 1) * TOK], jnp.zeros((8, TOK), F32)], axis=0)
                high = part.astype(BF16)
                low = (part - high.astype(F32)).astype(BF16)
                means = jnp.dot(high, weights, preferred_element_type=F32) + jnp.dot(
                    low, weights, preferred_element_type=F32
                )
                row = jnp.sum(jnp.where(diagonal, means, 0.0), axis=0, keepdims=True)
                result_send[t * (WIDE // TOK) + i, pl.ds(5, 1), :] = row
            return carry

        lax.fori_loop(0, NC * TOK // WIDE, one_tile, 0)

    def send_result(d):
        target = (cent_at(4 - d // 4, 4 - d % 4), p)
        send(result_send.at[d], result_recv.at[d], us.at[2], ur.at[2], target)

    def tile_of(t):
        return queries[pl.ds(pl.multiple_of(t * TILE, TILE), TILE), :]

    def scan(t, start, size, fresh):
        rows = cent[pl.ds(start * (CHUNK // 16), size // 16)].reshape(size, DIM)
        dots = lax.dot_general(rows, tile_of(t), (((1,), (1,)), ((), ())), preferred_element_type=F32)
        most = jnp.max(dots.reshape(size // 8, 8, TILE), axis=0)
        running[...] = jnp.maximum(most, jnp.where(fresh, -jnp.inf, running[...]))

    def close_tile(t):
        best = jnp.max(running[...], axis=0, keepdims=True)
        held = probed[pl.ds(pl.multiple_of(t * 64, 64), 64), :]
        found = lax.dot_general(held, tile_of(t), (((1,), (1,)), ((), ())), preferred_element_type=F32)
        for j in range(TILE // TOK):
            block = found[j * 16 : (j + 1) * 16, j * TOK : (j + 1) * TOK]
            pair = jnp.where(group8 == sub8 >> 2, block[:8], 0.0) + jnp.where(
                group8 - 2 == sub8 >> 2, block[8:], 0.0
            )
            four = pair + pltpu.roll(pair, 4, 0)
            result_send[t * (TILE // TOK) + j, pl.ds(0, 5), :] = jnp.where(
                sub8 < 4, four, jnp.broadcast_to(best[:, j * TOK : (j + 1) * TOK], (8, 128))
            )[:5]

    def first_step(i, carry):
        @pl.when(i == SUM_AT)
        def _():
            sum_rows()

        scan(0, i, CHUNK, i == 0)
        for k in range(4):
            collect_probed(4 * i + k)
        for k in range(2):
            collect_first(12 + 2 * lax.rem(i, 2) + k, 0)
        return carry

    running[...] = jnp.full((8, TILE), -jnp.inf, F32)
    lax.fori_loop(0, STEPS, first_step, 0)
    close_tile(0)

    def step(n, carry):
        s = 2 * n
        t, i = lax.div(s, STEPS), lax.rem(s, STEPS)

        @pl.when(s == STEPS)
        def _():
            arrived(queries.at[pl.ds(TILE, TILE)], qr.at[1])

        @pl.when(s == BUILD_AT)
        def _():
            await_line()
            build_passages()

        @pl.when(s == 2 * STEPS)
        def _():
            arrived(queries.at[pl.ds(2 * TILE, TILE)], qr.at[2])

        @pl.when(s == 3 * STEPS)
        def _():
            arrived(queries.at[pl.ds(3 * TILE, TILE)], qr.at[3])

        @pl.when(s == PRODUCTS_AT)
        def _():
            products()
            for d in (10, 9, 11, 6, 2, 5, 7, 8, 1, 3, 4):
                send_result(d)

        scan(t, i, 2 * CHUNK, i == 0)

        @pl.when(i == STEPS - 2)
        def _():
            close_tile(t)

        return carry

    lax.fori_loop(STEPS // 2, NC * TOK // TILE * STEPS // 2, step, 0)
    for d in (14, 13, 15, 12):
        send_result(d)

    place = lane8 & 31
    even = place < 16
    away = jnp.where(even, place >> 1, place - 16)
    base = lax.rem(z + 16 - away, 8) * (2 * P_OWN)
    base = jnp.where(place < 24, base, -1000)
    second = even & ((place & 1) == 1)
    nothing = [jnp.zeros((8, 128), F32) for _ in range(CMAX // 8)]

    def combine(cc, got, best, total, chosen):
        late = lax.rem(cc, 2)
        at = base + P_OWN * jnp.where(even, late, 1 - late) + jnp.where(second, P_OWN - 8 + lax.div(cc, 2), cc)
        scores = jnp.broadcast_to(got[5:6, :], (8, 128))
        chosen = [
            jnp.where(wanted[pl.ds(8 * g, 8), :] == at, scores, chosen[g]) for g in range(CMAX // 8)
        ]
        return jnp.maximum(best, got), total + got, chosen

    held = combine(c, result_send[0], jnp.full((8, 128), -jnp.inf, F32), jnp.zeros((8, 128), F32), nothing)
    gone(queries.at[pl.ds(0, 3 * TOK)], qs.at[0])
    for d in (1, 2, 3):
        gone(queries.at[pl.ds(0, TILE)], qs.at[d])
    gone(first_send.at[pl.ds(1, 3)], ws.at[0])
    gone(column_send.at[pl.ds(1, 3)], vs.at[0])

    @pl.when(odd == 0)
    def _():
        gone(second_send.at[1], ws.at[1])
        gone(late_send.at[pl.ds(1, 3)], vs.at[1])
        gone(passages.at[pl.ds(0, 7 * 64)], us.at[0])
        gone(passages.at[pl.ds(0, EVEN)], us.at[1])

    @pl.when(odd == 1)
    def _():
        gone(second_send, ws.at[1])
        gone(passages.at[pl.ds(EVEN, 7 * 32)], us.at[0])
        gone(passages.at[pl.ds(EVEN, 256)], us.at[1])

    gone(result_send.at[pl.ds(1, NC - 1)], us.at[2])
    arrived(result_recv.at[pl.ds(1, NC - 1)], ur.at[2])
    for d in range(1, NC):
        held = combine(cent_at(d // 4, d % 4), result_recv[d], *held)
    best, total, chosen = held
    chosen = jnp.concatenate(chosen, axis=0)
    ones = jnp.where(group8 == sub8, 1.0, 0.0).astype(BF16)
    scores = jnp.zeros((8, CMAX), F32)
    for _ in range(3):
        term = chosen.astype(BF16)
        scores += lax.dot_general(ones, term, (((1,), (1,)), ((), ())), preferred_element_type=F32)
        chosen = chosen - term.astype(F32)
    out[pl.ds(0, 8), :] = total
    out[pl.ds(4, 1), :] = best[4:5]
    out[pl.ds(8, 8), pl.ds(0, CMAX)] = scores


def deliver(got, top_out, probe_out, score_out):
    for q in range(QD):
        top_out[pl.ds(q, 1), :] = got[4:5, q * QT : (q + 1) * QT]
        probe_out[q] = got[:4, q * QT : (q + 1) * QT]
    score_out[...] = got[8 : 8 + QD, :CMAX]


def body(queries, probes, centroids, codebook, token_cells, codes, locations, candidates, lengths):
    vmem = pl.BlockSpec(memory_space=pltpu.VMEM)
    hbm = pl.BlockSpec(memory_space=pltpu.HBM)
    results = pl.pallas_call(
        kernel,
        out_shape=jax.ShapeDtypeStruct((16, 128), F32),
        in_specs=[hbm] * 9,
        out_specs=vmem,
        scratch_shapes=[
            pltpu.SMEM((NPROBE, NC * NP * QD), jnp.int32),
            pltpu.SMEM((P_OWN, PLEN), jnp.int32),
            pltpu.VMEM((P_OWN, 2, DIM), jnp.int32),
            pltpu.VMEM((4, DIM), F32),
            pltpu.SMEM((NP * P_OWN,), jnp.int32),
            pltpu.SMEM((QD, CMAX), jnp.int32),
            pltpu.SMEM((QD,), jnp.int32),
            pltpu.VMEM((SHARD // 16, 16, DIM), BF16),
            pltpu.VMEM((NC * TOK, DIM), BF16),
            pltpu.VMEM((4, 4, 32, DIM), BF16),
            pltpu.VMEM((4, 4, 32, DIM), BF16),
            pltpu.VMEM((2, 4, 32, DIM), BF16),
            pltpu.VMEM((4, 4, 32, DIM), BF16),
            pltpu.VMEM((4, 32, DIM), BF16),
            pltpu.VMEM((4, 32, DIM), BF16),
            pltpu.VMEM((4, 32, DIM), BF16),
            pltpu.VMEM((4, 32, DIM), BF16),
            pltpu.VMEM((NC * 16, DIM), BF16),
            pltpu.VMEM((EVEN + 256, DIM), BF16),
            pltpu.VMEM((NC, 8, 128), F32),
            pltpu.VMEM((NC, 8, 128), F32),
            pltpu.VMEM((CMAX, 128), jnp.int32),
            pltpu.VMEM((8, TILE), F32),
            pltpu.SemaphoreType.DMA((STEPS,)),
            pltpu.SemaphoreType.DMA((8,)),
            pltpu.SemaphoreType.REGULAR,
            pltpu.SemaphoreType.REGULAR,
        ]
        + [pltpu.SemaphoreType.DMA((4,))] * 8,
        compiler_params=pltpu.CompilerParams(
            collective_id=0, has_side_effects=True, vmem_limit_bytes=60 << 20
        ),
        name="late_interaction",
    )(
        queries.reshape(TOK, DIM), probes.T, token_cells, codes, codebook, locations, candidates, lengths,
        centroids.reshape(SHARD // 16, 16, DIM),
    )
    top, probe, score = pl.pallas_call(
        deliver,
        out_shape=(
            jax.ShapeDtypeStruct((QD, QT), F32),
            jax.ShapeDtypeStruct((QD, NPROBE, QT), F32),
            jax.ShapeDtypeStruct((QD, CMAX), F32),
        ),
        in_specs=[vmem],
        out_specs=[vmem] * 3,
        name="deliver",
    )(results)
    return top, jnp.transpose(probe, (0, 2, 1)), score


def solution(mesh):
    placed = (
        P(("cent", "pass"), None, None),
        P(),
        P("cent", None),
        P(),
        P("pass", None),
        P("pass", None, None),
        P(),
        P(("cent", "pass"), None),
        P(("cent", "pass")),
    )
    return jax.shard_map(
        body,
        mesh=mesh,
        in_specs=placed,
        out_specs=(
            P(("cent", "pass"), None),
            P(("cent", "pass"), None, None),
            P(("cent", "pass"), None),
        ),
        check_vma=False,
    )
```

```python
import jax
import jax.numpy as jnp
from jax import lax
from jax.experimental import pallas as pl
from jax.experimental.pallas import tpu as pltpu
from jax.sharding import PartitionSpec as P

MESH = pl.DeviceIdType.MESH
DIM = 128
QT = 32
NPROBE = 4
PLEN = 30
P_OWN = 24
CMAX = 40
NC = 16
NP = 16
QD = 4
TOK = QD * QT
SHARD = 16384
SHIFT = 14
CHUNK = 4096
TILE = 512
WIDE = 1024
STEPS = SHARD // CHUNK
SUM_AT = 2
BUILD_AT = 6
PRODUCTS_AT = 14
EVEN = 8 * 64
F32 = jnp.float32
BF16 = jnp.bfloat16


def kernel(
    q_hbm, probes_hbm, cells_hbm, codes_hbm, book_hbm, locations_hbm, candidates_hbm, lengths_hbm, cent_hbm,
    out,
    probes, cells, codes, book, locations, candidates, lengths,
    cent, queries, first_send, first_recv, second_send, second_recv, column_send, column_recv, late_send, late_recv,
    probed, passages, result_send, result_recv, wanted, running,
    load_sem, small_sem, plane_here, line_here, qs, qr, ws, wr, vs, vr, us, ur,
):
    c = lax.axis_index("cent")
    p = lax.axis_index("pass")
    y, x = lax.div(c, 4), lax.rem(c, 4)
    z, core = lax.div(p, 2), lax.rem(p, 2)
    odd = lax.rem(c + p, 2)
    second_of = P_OWN - 8 + lax.div(c, 2)

    def cent_at(dy, dx):
        return lax.rem(y + dy, 4) * 4 + lax.rem(x + dx, 4)

    def pass_at(dz):
        return lax.rem(z + dz, 8) * 2 + core

    other = z * 2 + 1 - core

    loads = [
        pltpu.make_async_copy(
            cent_hbm.at[pl.ds(i * CHUNK // 16, CHUNK // 16)], cent.at[pl.ds(i * CHUNK // 16, CHUNK // 16)], load_sem.at[i]
        )
        for i in range(SHARD // CHUNK)
    ]
    small = [
        pltpu.make_async_copy(src, dst, small_sem.at[i])
        for i, (src, dst) in enumerate(
            (
                (q_hbm, queries.at[pl.ds(0, TOK)]),
                (cells_hbm, cells),
                (probes_hbm, probes),
                (codes_hbm, codes),
                (book_hbm, book),
                (locations_hbm, locations),
                (candidates_hbm, candidates),
                (lengths_hbm, lengths),
            )
        )
    ]
    for load in small + loads:
        load.start()

    barrier = pltpu.get_barrier_semaphore()
    for d in (2, 1, 3):
        for there in (cent_at(0, d), cent_at(d, 0)):
            pl.semaphore_signal(barrier, inc=1, device_id=(there, z * 2), device_id_type=MESH)
    for d in range(1, 8):
        pl.semaphore_signal(
            barrier, inc=1, device_id=(c, lax.rem(z + d, 8) * 2 + 1), device_id_type=MESH
        )

    @pl.when(core == 1)
    def _():
        pl.semaphore_signal(barrier, inc=1, device_id=(c, other), device_id_type=MESH)
        pl.semaphore_wait(plane_here, 1)

    @pl.when(core == 0)
    def _():
        pl.semaphore_wait(barrier, 13)
        pl.semaphore_signal(plane_here, inc=1, device_id=(c, other), device_id_type=MESH)

    small[0].wait()
    lane8 = lax.broadcasted_iota(jnp.int32, (8, 128), 1)
    sub8 = lax.broadcasted_iota(jnp.int32, (8, 128), 0)

    def send(src, dst, send_sem, recv_sem, target):
        pltpu.make_async_remote_copy(
            src_ref=src, dst_ref=dst, send_sem=send_sem, recv_sem=recv_sem, device_id=target, device_id_type=MESH
        ).start()

    def arrived(ref, sem):
        pltpu.make_async_remote_copy(
            src_ref=ref, dst_ref=ref, send_sem=sem, recv_sem=sem, device_id=(c, other), device_id_type=MESH
        ).wait_recv()

    def gone(ref, sem):
        pltpu.make_async_remote_copy(
            src_ref=ref, dst_ref=ref, send_sem=sem, recv_sem=sem, device_id=(c, other), device_id_type=MESH
        ).wait_send()

    for d in (1, 3, 2):
        send(queries.at[pl.ds(0, TOK)], queries.at[pl.ds(d * TOK, TOK)], qs.at[0], qr.at[0], (cent_at(0, d), p))
    for load in small[1:] + loads:
        load.wait()

    mine = [jnp.where(sub8 == r, c, -1) for r in range(8)]

    def pick(ids):
        parts = []
        for base in range(0, len(ids), 8):
            acc = jnp.zeros((8, DIM), F32)
            for r, i in enumerate(ids[base : base + 8]):
                pair = cent[(i & (SHARD - 1)) >> 4].astype(F32)
                ids_r = jnp.full((8, DIM), i, jnp.int32)
                half = jnp.where((ids_r & 8) != 0, pair[8:], pair[:8])
                row = jnp.take_along_axis(half, ids_r & 7, axis=0)
                acc = jnp.where(mine[r] == (ids_r >> SHIFT), row, acc)
            parts.append(acc)
        return jnp.concatenate(parts, axis=0).astype(BF16)

    def collect_first(i, carry):
        dx, dy = lax.rem(lax.div(i, 4) + 1, 4), lax.rem(i, 4)
        target = cent_at(4 - dy, 4 - dx)
        first_send[dx, dy] = pick([cells[target, min(j, PLEN - 1)] for j in range(32)])
        return carry

    def collect_second(i, carry):
        half, dy = lax.div(i, 4), lax.rem(i, 4)
        at = P_OWN - 8 + lax.div(cent_at(4 - dy, 4 - 2 * half - odd), 2)
        second_send[half, dy] = pick([cells[at, min(j, PLEN - 1)] for j in range(32)])
        return carry

    def collect_probed(d):
        base = (cent_at(4 - lax.div(d, 4), 4 - lax.rem(d, 4)) * NP + p) * QD
        probed[pl.ds(pl.multiple_of(d * 16, 16), 16), :] = pick(
            [probes[k, base + q] for q in range(QD) for k in range(NPROBE)]
        )

    lax.fori_loop(0, 12, collect_first, 0)
    for d in (1, 3, 2):
        send(first_send.at[d], first_recv.at[d], ws.at[0], wr.at[0], (cent_at(0, 4 - d), p))
    lax.fori_loop(0, 8, collect_second, 0)

    def send_second(half, d):
        send(second_send.at[half], second_recv.at[d], ws.at[1], wr.at[1], (cent_at(0, 4 - d), p))

    @pl.when(odd == 0)
    def _():
        send_second(1, 2)

    @pl.when(odd == 1)
    def _():
        send_second(0, 1)
        send_second(1, 3)

    arrived(queries.at[pl.ds(TOK, 3 * TOK)], qr.at[0])
    for d in (1, 3, 2):
        send(queries.at[pl.ds(0, TILE)], queries.at[pl.ds(d * TILE, TILE)], qs.at[d], qr.at[d], (cent_at(d, 0), p))

    group8 = lane8 >> 5
    for base in range(0, CMAX, 8):
        found = jnp.full((8, 128), -1, jnp.int32)
        for q in range(QD):
            for r in range(8):
                at = locations[candidates[q, base + r]]
                found = jnp.where((sub8 == r) & (group8 == q), at, found)
            live = base + sub8 < lengths[q]
            found = jnp.where((group8 == q) & jnp.logical_not(live), -1, found)
        wanted[pl.ds(base, 8), :] = found

    def sum_rows():
        arrived(first_recv.at[pl.ds(1, 3)], wr.at[0])
        for dy in range(4):
            total = first_send[0, dy].astype(F32)
            for d in (1, 2, 3):
                total += first_recv[d, dy].astype(F32)
            column_send[dy] = total.astype(BF16)
        for dy in (1, 3, 2):
            send(column_send.at[dy], column_recv.at[dy], vs.at[0], vr.at[0], (cent_at(4 - dy, 0), p))

        @pl.when(odd == 0)
        def _():
            arrived(second_recv.at[pl.ds(1, 3)], wr.at[1])
            for dy in range(4):
                total = second_send[0, dy].astype(F32)
                for d in (1, 2, 3):
                    total += second_recv[d, dy].astype(F32)
                late_send[dy] = total.astype(BF16)
            for dy in (1, 3, 2):
                send(late_send.at[dy], late_recv.at[dy], vs.at[1], vr.at[1], (cent_at(4 - dy, 0), p))

    def decode(parts, at):
        rows = sum(parts[1:], parts[0])
        token = jnp.minimum(lax.broadcasted_iota(jnp.int32, (32, DIM), 0), PLEN - 1)
        shift = 2 * jnp.where(token >= 15, token - 15, token)
        words = codes[at]
        word = jnp.where(token >= 15, words[1:2, :], words[0:1, :])
        level = jnp.right_shift(word, shift) & 3
        residual = jnp.where(
            level < 2,
            jnp.where(level == 0, book[0:1, :], book[1:2, :]),
            jnp.where(level == 2, book[2:3, :], book[3:4, :]),
        )
        vector = rows + residual
        squares = jnp.sum(vector * vector, axis=-1, keepdims=True)
        return (vector * lax.rsqrt(squares + 1e-06)).astype(BF16)

    def await_line():
        @pl.when(core == 1)
        def _():
            pl.semaphore_wait(barrier, 14)
            pl.semaphore_signal(line_here, inc=1, device_id=(c, other), device_id_type=MESH)

        @pl.when(core == 0)
        def _():
            pl.semaphore_wait(line_here, 1)

    def send_passages(start, size, d, near):
        i = 0 if near else 1
        there = pass_at(d) if near else lax.rem(z + d, 8) * 2 + 1 - core
        send(
            passages.at[pl.ds(start, size)], passages.at[pl.ds(start + d * size, size)], us.at[i], ur.at[i], (c, there)
        )

    def build_passages():
        arrived(column_recv.at[pl.ds(1, 3)], vr.at[0])
        built = decode([column_send[0].astype(F32)] + [column_recv[d].astype(F32) for d in (1, 2, 3)], c)

        @pl.when(odd == 0)
        def _():
            arrived(late_recv.at[pl.ds(1, 3)], vr.at[1])
            passages[pl.ds(0, 32), :] = built
            passages[pl.ds(32, 32), :] = decode(
                [late_send[0].astype(F32)] + [late_recv[d].astype(F32) for d in (1, 2, 3)], second_of
            )
            for d in (4, 3, 5, 2, 6, 1, 7, 0):
                for near in ((True, False) if d else (False,)):
                    send_passages(0, 64, d, near)

        @pl.when(odd == 1)
        def _():
            passages[pl.ds(EVEN, 32), :] = built
            for d in (4, 3, 5, 2, 6, 1, 7, 0):
                for near in ((True, False) if d else (False,)):
                    send_passages(EVEN, 32, d, near)

    def products():
        @pl.when(odd == 0)
        def _():
            arrived(passages.at[pl.ds(64, EVEN - 64)], ur.at[0])
            arrived(passages.at[pl.ds(EVEN, 256)], ur.at[1])

        @pl.when(odd == 1)
        def _():
            arrived(passages.at[pl.ds(EVEN + 32, 224)], ur.at[0])
            arrived(passages.at[pl.ds(0, EVEN)], ur.at[1])

        lane = lax.broadcasted_iota(jnp.int32, (TOK, 128), 1)
        token = lax.broadcasted_iota(jnp.int32, (TOK, 128), 0)
        weights = jnp.where(lane >> 5 == token >> 5, 1.0 / QT, 0.0).astype(BF16)
        diagonal = ((lane & 31) == (token & 31))[:32]

        def one_tile(t, carry):
            tile = queries[pl.ds(pl.multiple_of(t * WIDE, WIDE), WIDE), :]
            dots = lax.dot_general(passages[...], tile, (((1,), (1,)), ((), ())), preferred_element_type=F32)
            most = jnp.max(dots.reshape(24, 32, WIDE), axis=1)
            for i in range(WIDE // TOK):
                part = jnp.concatenate([most[:, i * TOK : (i + 1) * TOK], jnp.zeros((8, TOK), F32)], axis=0)
                high = part.astype(BF16)
                low = (part - high.astype(F32)).astype(BF16)
                means = jnp.dot(high, weights, preferred_element_type=F32) + jnp.dot(
                    low, weights, preferred_element_type=F32
                )
                row = jnp.sum(jnp.where(diagonal, means, 0.0), axis=0, keepdims=True)
                result_send[t * (WIDE // TOK) + i, pl.ds(5, 1), :] = row
            return carry

        lax.fori_loop(0, NC * TOK // WIDE, one_tile, 0)

    def send_result(d):
        target = (cent_at(4 - d // 4, 4 - d % 4), p)
        send(result_send.at[d], result_recv.at[d], us.at[2], ur.at[2], target)

    def tile_of(t):
        return queries[pl.ds(pl.multiple_of(t * TILE, TILE), TILE), :]

    def scan(t, start, size, fresh):
        rows = cent[pl.ds(start * (CHUNK // 16), size // 16)].reshape(size, DIM)
        dots = lax.dot_general(rows, tile_of(t), (((1,), (1,)), ((), ())), preferred_element_type=F32)
        most = jnp.max(dots.reshape(size // 8, 8, TILE), axis=0)
        running[...] = jnp.maximum(most, jnp.where(fresh, -jnp.inf, running[...]))

    def close_tile(t):
        best = jnp.max(running[...], axis=0, keepdims=True)
        held = probed[pl.ds(pl.multiple_of(t * 64, 64), 64), :]
        found = lax.dot_general(held, tile_of(t), (((1,), (1,)), ((), ())), preferred_element_type=F32)
        for j in range(TILE // TOK):
            block = found[j * 16 : (j + 1) * 16, j * TOK : (j + 1) * TOK]
            pair = jnp.where(group8 == sub8 >> 2, block[:8], 0.0) + jnp.where(
                group8 - 2 == sub8 >> 2, block[8:], 0.0
            )
            four = pair + pltpu.roll(pair, 4, 0)
            result_send[t * (TILE // TOK) + j, pl.ds(0, 5), :] = jnp.where(
                sub8 < 4, four, jnp.broadcast_to(best[:, j * TOK : (j + 1) * TOK], (8, 128))
            )[:5]

    def first_step(i, carry):
        @pl.when(i == SUM_AT // 2)
        def _():
            sum_rows()

        scan(0, 2 * i, 2 * CHUNK, i == 0)
        for k in range(8):
            collect_probed(8 * i + k)
        for k in range(4):
            collect_first(12 + k, 0)
        return carry

    running[...] = jnp.full((8, TILE), -jnp.inf, F32)
    lax.fori_loop(0, STEPS // 2, first_step, 0)
    close_tile(0)

    def step(n, carry):
        s = 2 * n
        t, i = lax.div(s, STEPS), lax.rem(s, STEPS)

        @pl.when(s == STEPS)
        def _():
            arrived(queries.at[pl.ds(TILE, TILE)], qr.at[1])

        @pl.when(s == BUILD_AT)
        def _():
            await_line()
            build_passages()

        @pl.when(s == 2 * STEPS)
        def _():
            arrived(queries.at[pl.ds(2 * TILE, TILE)], qr.at[2])

        @pl.when(s == 3 * STEPS)
        def _():
            arrived(queries.at[pl.ds(3 * TILE, TILE)], qr.at[3])

        @pl.when(s == PRODUCTS_AT)
        def _():
            products()
            for d in (10, 9, 11, 6, 2, 5, 7, 8, 1, 3, 4):
                send_result(d)

        scan(t, i, 2 * CHUNK, i == 0)

        @pl.when(i == STEPS - 2)
        def _():
            close_tile(t)

        return carry

    lax.fori_loop(STEPS // 2, NC * TOK // TILE * STEPS // 2, step, 0)
    for d in (14, 13, 15, 12):
        send_result(d)

    place = lane8 & 31
    even = place < 16
    away = jnp.where(even, place >> 1, place - 16)
    base = lax.rem(z + 16 - away, 8) * (2 * P_OWN)
    base = jnp.where(place < 24, base, -1000)
    second = even & ((place & 1) == 1)
    nothing = [jnp.zeros((8, 128), F32) for _ in range(CMAX // 8)]

    def combine(cc, got, best, total, chosen):
        late = lax.rem(cc, 2)
        at = base + P_OWN * jnp.where(even, late, 1 - late) + jnp.where(second, P_OWN - 8 + lax.div(cc, 2), cc)
        scores = jnp.broadcast_to(got[5:6, :], (8, 128))
        chosen = [
            jnp.where(wanted[pl.ds(8 * g, 8), :] == at, scores, chosen[g]) for g in range(CMAX // 8)
        ]
        return jnp.maximum(best, got), total + got, chosen

    held = combine(c, result_send[0], jnp.full((8, 128), -jnp.inf, F32), jnp.zeros((8, 128), F32), nothing)
    gone(queries.at[pl.ds(0, 3 * TOK)], qs.at[0])
    for d in (1, 2, 3):
        gone(queries.at[pl.ds(0, TILE)], qs.at[d])
    gone(first_send.at[pl.ds(1, 3)], ws.at[0])
    gone(column_send.at[pl.ds(1, 3)], vs.at[0])

    @pl.when(odd == 0)
    def _():
        gone(second_send.at[1], ws.at[1])
        gone(late_send.at[pl.ds(1, 3)], vs.at[1])
        gone(passages.at[pl.ds(0, 7 * 64)], us.at[0])
        gone(passages.at[pl.ds(0, EVEN)], us.at[1])

    @pl.when(odd == 1)
    def _():
        gone(second_send, ws.at[1])
        gone(passages.at[pl.ds(EVEN, 7 * 32)], us.at[0])
        gone(passages.at[pl.ds(EVEN, 256)], us.at[1])

    gone(result_send.at[pl.ds(1, NC - 1)], us.at[2])
    arrived(result_recv.at[pl.ds(1, NC - 1)], ur.at[2])
    for d in range(1, NC):
        held = combine(cent_at(d // 4, d % 4), result_recv[d], *held)
    best, total, chosen = held
    chosen = jnp.concatenate(chosen, axis=0)
    ones = jnp.where(group8 == sub8, 1.0, 0.0).astype(BF16)
    scores = jnp.zeros((8, CMAX), F32)
    for _ in range(3):
        term = chosen.astype(BF16)
        scores += lax.dot_general(ones, term, (((1,), (1,)), ((), ())), preferred_element_type=F32)
        chosen = chosen - term.astype(F32)
    out[pl.ds(0, 8), :] = total
    out[pl.ds(4, 1), :] = best[4:5]
    out[pl.ds(8, 8), pl.ds(0, CMAX)] = scores


def deliver(got, top_out, probe_out, score_out):
    for q in range(QD):
        top_out[pl.ds(q, 1), :] = got[4:5, q * QT : (q + 1) * QT]
        probe_out[q] = got[:4, q * QT : (q + 1) * QT]
    score_out[...] = got[8 : 8 + QD, :CMAX]


def body(queries, probes, centroids, codebook, token_cells, codes, locations, candidates, lengths):
    vmem = pl.BlockSpec(memory_space=pltpu.VMEM)
    hbm = pl.BlockSpec(memory_space=pltpu.HBM)
    results = pl.pallas_call(
        kernel,
        out_shape=jax.ShapeDtypeStruct((16, 128), F32),
        in_specs=[hbm] * 9,
        out_specs=vmem,
        scratch_shapes=[
            pltpu.SMEM((NPROBE, NC * NP * QD), jnp.int32),
            pltpu.SMEM((P_OWN, PLEN), jnp.int32),
            pltpu.VMEM((P_OWN, 2, DIM), jnp.int32),
            pltpu.VMEM((4, DIM), F32),
            pltpu.SMEM((NP * P_OWN,), jnp.int32),
            pltpu.SMEM((QD, CMAX), jnp.int32),
            pltpu.SMEM((QD,), jnp.int32),
            pltpu.VMEM((SHARD // 16, 16, DIM), BF16),
            pltpu.VMEM((NC * TOK, DIM), BF16),
            pltpu.VMEM((4, 4, 32, DIM), BF16),
            pltpu.VMEM((4, 4, 32, DIM), BF16),
            pltpu.VMEM((2, 4, 32, DIM), BF16),
            pltpu.VMEM((4, 4, 32, DIM), BF16),
            pltpu.VMEM((4, 32, DIM), BF16),
            pltpu.VMEM((4, 32, DIM), BF16),
            pltpu.VMEM((4, 32, DIM), BF16),
            pltpu.VMEM((4, 32, DIM), BF16),
            pltpu.VMEM((NC * 16, DIM), BF16),
            pltpu.VMEM((EVEN + 256, DIM), BF16),
            pltpu.VMEM((NC, 8, 128), F32),
            pltpu.VMEM((NC, 8, 128), F32),
            pltpu.VMEM((CMAX, 128), jnp.int32),
            pltpu.VMEM((8, TILE), F32),
            pltpu.SemaphoreType.DMA((STEPS,)),
            pltpu.SemaphoreType.DMA((8,)),
            pltpu.SemaphoreType.REGULAR,
            pltpu.SemaphoreType.REGULAR,
        ]
        + [pltpu.SemaphoreType.DMA((4,))] * 8,
        compiler_params=pltpu.CompilerParams(
            collective_id=0, has_side_effects=True, vmem_limit_bytes=60 << 20
        ),
        name="late_interaction",
    )(
        queries.reshape(TOK, DIM), probes.T, token_cells, codes, codebook, locations, candidates, lengths,
        centroids.reshape(SHARD // 16, 16, DIM),
    )
    top, probe, score = pl.pallas_call(
        deliver,
        out_shape=(
            jax.ShapeDtypeStruct((QD, QT), F32),
            jax.ShapeDtypeStruct((QD, NPROBE, QT), F32),
            jax.ShapeDtypeStruct((QD, CMAX), F32),
        ),
        in_specs=[vmem],
        out_specs=[vmem] * 3,
        name="deliver",
    )(results)
    return top, jnp.transpose(probe, (0, 2, 1)), score


def solution(mesh):
    placed = (
        P(("cent", "pass"), None, None),
        P(),
        P("cent", None),
        P(),
        P("pass", None),
        P("pass", None, None),
        P(),
        P(("cent", "pass"), None),
        P(("cent", "pass")),
    )
    return jax.shard_map(
        body,
        mesh=mesh,
        in_specs=placed,
        out_specs=(
            P(("cent", "pass"), None),
            P(("cent", "pass"), None, None),
            P(("cent", "pass"), None),
        ),
        check_vma=False,
    )
```
